256 devices in a mesh: pts: 64 (over x, z, core), rep: 4 (over y).
Axes of the slice: x: 4, y: 4, z: 8, core: 2. Of those that a mesh axis runs over, the one named last changes fastest.
Arguments:
- points: bfloat16 [131072, 256], P('pts'), may hold values from -6 to 6
- counts: int32 [64], P('pts'), may hold values from 1024 to 2048, as said below
- order: int32 [131072], P('pts'), may hold values from 0 to 2047, as said below
- grad_out: bfloat16 [131072, 256], P('pts'), may hold values from -6 to 6
- w_qkv: bfloat16 [3, 256, 256], P(None, None, 'rep'), may hold values from -1 to 1
- w_proj: bfloat16 [256, 256], P('rep'), may hold values from -0.375 to 0.375
Outputs:
- out: bfloat16 [131072, 256], P('pts', 'rep')
- grad_input: float32 [131072, 256], P('pts', 'rep')
- grad_qkv: float32 [3, 256, 256], P(None, None, 'rep')
- grad_proj: float32 [256, 256], P('rep')
The draws below stay inside these ranges and needn't reach their ends.
Inputs may be any that keep to these rules, and one draw needn't show every extreme that they name: `counts`: live points of each device; some device has all 2048. `order`: each device's 2048 entries are a permutation of its local slots.
All inputs are finite; a program needn't handle non-finite values.
Results may differ from the reference program's by a relative error of at most 0.011.
Values may be sent and summed in bfloat16 or wider, within the bound.
A program may use at most 64 MiB of HBM per device.

```python
import jax
import jax.numpy as jnp
from jax import lax

C = 256
HEADS = 16
PATCH = 512
HEAD = 16
P_DEV = 2048
SOURCES = 64
POINTS = 131072


def draw_counts(key, part):
    key = jax.random.fold_in(key, 11)
    first, second = jax.random.split(key)
    values = jax.random.randint(first, (SOURCES,), P_DEV // 2, P_DEV + 1)
    fullest = jax.random.randint(second, (), 0, SOURCES)
    return values.at[fullest].set(P_DEV).astype(jnp.int32)


def draw_order(key, part):
    key = jax.random.fold_in(key, 23)
    keys = jax.random.split(key, SOURCES)
    perms = jax.vmap(lambda k: jax.random.permutation(k, P_DEV))(keys)
    return perms.reshape(-1).astype(jnp.int32)


def rising_rows(top):
    position = jnp.arange(C, dtype=jnp.float32) / jnp.float32(C - 1)
    scales = jnp.exp(position * jnp.log(jnp.float32(top)))
    return scales / jnp.sqrt(jnp.mean(scales * scales))


def draw_w_qkv(key, part):
    key = jax.random.fold_in(key, 37)
    first, second = jax.random.split(key)
    noise = jnp.clip(jax.random.normal(first, (3, C, C), jnp.float32), -4.0, 4.0)
    common = jnp.clip(jax.random.normal(second, (3, 1, C), jnp.float32), -4.0, 4.0)
    scales = rising_rows(8.0)
    values = scales[None, :, None] * (noise + 0.7 * common) / jnp.sqrt(jnp.float32(C))
    return jnp.clip(values, -1.0, 1.0).astype(jnp.bfloat16)


def block_levels(stream_key, shape, cuts, low, top_value):
    factor_of = 1.0
    for dim, blocks in cuts:
        heights = jax.random.uniform(jax.random.fold_in(jax.random.fold_in(stream_key, 6), dim), (blocks,), jnp.float32, low / len(cuts), top_value / len(cuts))
        factor_of = factor_of * jnp.repeat(jnp.exp(heights), shape[dim] // blocks).reshape((-1,) + (1,) * (len(shape) - 1 - dim))
    return factor_of


def normal_values(rng, extent, deviation, bound, shards=(), kind=jnp.bfloat16):
    values = jax.random.normal(rng, extent, jnp.float32) * deviation
    if len(shards) > 0:
        values = block_levels(rng, extent, shards, -0.22, 0.18) * values
    return jnp.clip(values, min=-bound, max=bound).astype(kind)


def setup_inputs(seed: int = 0) -> dict:
    splits = jax.random.split(jax.random.key(seed), 7)
    points = normal_values(splits[0], (POINTS, C), 1.0, 6.0, ((0, 64),))
    counts = draw_counts(jax.random.fold_in(splits[6], 71), 0)
    order = draw_order(jax.random.fold_in(splits[6], 71), 0)
    grad_out = normal_values(splits[3], (POINTS, C), 1.0, 6.0, ((0, 64),))
    w_qkv = draw_w_qkv(jax.random.fold_in(splits[6], 71), 0)
    w_proj = normal_values(splits[5], (C, C), C ** -0.5, 0.375, ((0, 4),))
    return dict(points=points, counts=counts, order=order, grad_out=grad_out, w_qkv=w_qkv, w_proj=w_proj)


SCALE = 0.25
EPS = 1e-05
NEGATIVE = -1e+30

def regroup(array, order, count):
    slots = array.shape[0] // count
    blocks = array.reshape((count, slots) + array.shape[1:])
    index = order.reshape(count, slots)
    moved = jax.vmap(lambda block, where: block[where])(blocks, index)
    moved = moved.reshape((count, count, slots // count) + array.shape[1:])
    moved = jnp.swapaxes(moved, 0, 1)
    return moved.reshape(array.shape)

def ungroup(array, order, count):
    slots = array.shape[0] // count
    moved = array.reshape((count, count, slots // count) + array.shape[1:])
    moved = jnp.swapaxes(moved, 0, 1).reshape((count, slots) + array.shape[1:])
    index = order.reshape(count, slots)
    back = jax.vmap(lambda block, where: block[jnp.argsort(where)])(moved, index)
    return back.reshape(array.shape)

def head_probs(query, key_rows, keep):
    scores = jnp.einsum('pld,pmd->plm', query.astype(jnp.float32), key_rows.astype(jnp.float32)) * SCALE
    length = scores.shape[1]
    allowed = keep[:, None, :] | jnp.eye(length, dtype=bool)[None]
    scores = jnp.where(allowed, scores, NEGATIVE)
    peak = lax.optimization_barrier(jnp.max(scores, axis=-1, keepdims=True))
    expo = jnp.exp(scores - peak)
    return expo / lax.optimization_barrier(jnp.sum(expo, axis=-1, keepdims=True))

def head_forward(query, key_rows, values, keep):
    probs = head_probs(query, key_rows, keep).astype(jnp.bfloat16)
    return jnp.einsum('plm,pmd->pld', probs.astype(jnp.float32), values.astype(jnp.float32))

def head_backward(query, key_rows, values, keep, d_attn):
    probs = head_probs(query, key_rows, keep)
    rounded = probs.astype(jnp.bfloat16).astype(jnp.float32)
    d_attn = d_attn.astype(jnp.float32)
    d_probs = jnp.einsum('pld,pmd->plm', d_attn, values.astype(jnp.float32))
    d_values = jnp.einsum('plm,pld->pmd', rounded, d_attn)
    d_scores = probs * (d_probs - lax.optimization_barrier(jnp.sum(d_probs * probs, axis=-1, keepdims=True))) * SCALE
    d_scores = d_scores.astype(jnp.bfloat16).astype(jnp.float32)
    d_query = jnp.einsum('plm,pmd->pld', d_scores, key_rows.astype(jnp.float32))
    d_keys = jnp.einsum('plm,pld->pmd', d_scores, query.astype(jnp.float32))
    return (d_query, d_keys, d_values)

def forward_heads(query, key_rows, values, keep):
    stacked = tuple((jnp.moveaxis(t, 2, 0) for t in (query, key_rows, values)))
    result = lax.map(lambda t: head_forward(t[0], t[1], t[2], keep), stacked)
    return jnp.moveaxis(result, 0, 2)

def backward_heads(query, key_rows, values, keep, d_attn):
    stacked = tuple((jnp.moveaxis(t, 2, 0) for t in (query, key_rows, values, d_attn)))
    result = lax.map(lambda t: head_backward(t[0], t[1], t[2], keep, t[3]), stacked)
    return tuple((jnp.moveaxis(r, 0, 2) for r in result))

def reference(points, counts, order, grad_out, w_qkv, w_proj):
    count = SOURCES
    live = (jnp.arange(P_DEV)[None, :] < counts[:, None]).reshape(-1).astype(jnp.int32)
    xs = regroup(points, order, count)
    gs = regroup(grad_out, order, count)
    keep = regroup(live, order, count) > 0
    rows = xs.shape[0]
    input_float32 = xs.astype(jnp.float32)
    centered_values = lax.optimization_barrier(jnp.mean(input_float32, axis=1, keepdims=True))
    spread = lax.optimization_barrier(jnp.mean((input_float32 - centered_values) ** 2, axis=1, keepdims=True))
    inverse_deviation = 1.0 / jnp.sqrt(spread + EPS)
    standardized_input = (input_float32 - centered_values) * inverse_deviation
    normalized_input = standardized_input.astype(jnp.bfloat16)
    parts = [jnp.dot(normalized_input, w_qkv[i], preferred_element_type=jnp.float32).astype(jnp.bfloat16) for i in range(3)]
    shaped = [t.reshape(rows // PATCH, 1, PATCH, HEADS, HEAD) for t in parts]
    keep_patch = keep.reshape(rows // PATCH, 1, PATCH)
    attn = lax.map(lambda t: forward_heads(t[0], t[1], t[2], t[3]), (shaped[0], shaped[1], shaped[2], keep_patch))
    attn = attn.reshape(rows, C).astype(jnp.bfloat16)
    mixed = jnp.dot(attn, w_proj, preferred_element_type=jnp.float32)
    livef = keep.astype(jnp.float32)[:, None]
    outs = (livef * (input_float32 + mixed)).astype(jnp.bfloat16)
    output_gradient = livef * gs.astype(jnp.float32)
    grad_yb = output_gradient.astype(jnp.bfloat16)
    grad_proj = jnp.dot(attn.T, grad_yb, preferred_element_type=jnp.float32)
    d_attn = jnp.dot(grad_yb, w_proj.T, preferred_element_type=jnp.float32).astype(jnp.bfloat16)
    d_shaped = d_attn.reshape(rows // PATCH, 1, PATCH, HEADS, HEAD)
    grads = lax.map(lambda t: backward_heads(t[0], t[1], t[2], t[3], t[4]), (shaped[0], shaped[1], shaped[2], keep_patch, d_shaped))
    grads = [g.reshape(rows, C).astype(jnp.bfloat16) for g in grads]
    grad_qkv = jnp.stack([jnp.dot(normalized_input.T, grads[i], preferred_element_type=jnp.float32) for i in range(3)])
    normalized_gradient = grads[0].astype(jnp.float32) * 0.0
    for i in range(3):
        normalized_gradient = normalized_gradient + jnp.dot(grads[i], w_qkv[i].T, preferred_element_type=jnp.float32)
    mean_gradient = lax.optimization_barrier(jnp.mean(normalized_gradient, axis=1, keepdims=True))
    projected_mean_gradient = lax.optimization_barrier(jnp.mean(normalized_gradient * standardized_input, axis=1, keepdims=True))
    point_gradient = output_gradient + inverse_deviation * (normalized_gradient - mean_gradient - standardized_input * projected_mean_gradient)
    return (ungroup(outs, order, count), ungroup(point_gradient, order, count), grad_qkv, grad_proj)
```

```python
import functools

import jax
import jax.numpy as jnp
from jax import lax
from jax.experimental import pallas as pl
from jax.experimental.pallas import tpu as pltpu
from jax.sharding import PartitionSpec as P

HEAD = 16
CORES = 2
SCALE = 0.25
EPS = 1e-05
NEGATIVE = -1e30
DEAD = 64.0
ALIVE_BELOW = 32.0
F32, BF16 = jnp.float32, jnp.bfloat16
MESH = pl.DeviceIdType.MESH
VMEM = pl.BlockSpec(memory_space=pltpu.VMEM)
SMEM = pl.BlockSpec(memory_space=pltpu.SMEM)


def dot(a, b, ca=1, cb=0):
    return lax.dot_general(a, b, (((ca,), (cb,)), ((), ())), preferred_element_type=F32)


def column(row):
    wide = jnp.broadcast_to(row.astype(F32), (8, row.shape[1]))
    return wide.T[:, 0:1].astype(jnp.int32)


def greet(peers):
    barrier = pltpu.get_barrier_semaphore()
    for peer in peers:
        pl.semaphore_signal(barrier, inc=1, device_id=peer, device_id_type=MESH)
    pl.semaphore_wait(barrier, len(peers))


def send(src, dst, send_sem, recv_sem, peer):
    copy = pltpu.make_async_remote_copy(
        src_ref=src, dst_ref=dst, send_sem=send_sem, recv_sem=recv_sem,
        device_id=peer, device_id_type=MESH,
    )
    copy.start()
    return copy


def gather_kernel(
    reps, group, points_ref, grads_ref, order_ref, counts_ref, w_ref, wp_ref,
    x_ref, g_ref, w_all_ref, wp_all_ref,
    xs, gs, w_sems, wp_sems, x_sems, g_sems,
):
    me, rep = lax.axis_index("pts"), lax.axis_index("rep")
    member = lax.rem(me, group)
    base = me - member
    slots = points_ref.shape[0]
    patch = x_ref.shape[0]
    block = patch // group
    width = wp_ref.shape[0]
    beside = [(me, lax.rem(rep + k, reps)) for k in range(1, reps)]
    along = [lax.rem(member + k, group) for k in range(1, group)]
    greet(beside + [(base + other, rep) for other in along])

    copies = []
    mine = pl.ds(pl.multiple_of(rep * width, width), width)
    for k, peer in enumerate(beside):
        copies.append(send(w_ref, w_all_ref.at[:, mine, :], w_sems.at[0, k], w_sems.at[1, k], peer))
        copies.append(send(wp_ref, wp_all_ref.at[mine, :], wp_sems.at[0, k], wp_sems.at[1, k], peer))
    w_all_ref[:, mine, :] = w_ref[...]
    wp_all_ref[mine, :] = wp_ref[...]

    rows = column(order_ref[:, pl.ds(pl.multiple_of(rep * patch, patch), patch)])
    live = rows < counts_ref[0]
    slot = lax.broadcasted_iota(jnp.int32, (patch, slots), 1)
    pick = jnp.where(rows == slot, 1.0, 0.0).astype(BF16)
    here = pl.ds(pl.multiple_of(member * block, block), block)
    for source, dead, staged, landed, sems in (
        (points_ref, DEAD, xs, x_ref, x_sems),
        (grads_ref, 0.0, gs, g_ref, g_sems),
    ):
        staged[...] = jnp.where(live, dot(pick, source[...]), dead).astype(BF16)
        for k, other in enumerate(along):
            there = pl.ds(pl.multiple_of(other * block, block), block)
            copies.append(
                send(staged.at[there, :], landed.at[here, :], sems.at[0, k], sems.at[1, k], (base + other, rep))
            )
        landed[here, :] = staged[here, :]
    for copy in copies:
        copy.wait()


def attention_kernel(
    reps, x_ref, g_ref, w_ref, wp_ref, pay_ref, grad_ref, qkv, da, bias, at, dqkv, hbuf
):
    patch, channels = x_ref.shape
    width = channels // reps
    x = x_ref[...].astype(F32)
    mu = jnp.mean(x, axis=1, keepdims=True)
    centered = x - mu
    var = jnp.mean(centered * centered, axis=1, keepdims=True)
    inv = lax.rsqrt(var + EPS)
    hbuf[...] = (centered * inv).astype(BF16)
    keep = x[:, 0:1] < ALIVE_BELOW
    weights = w_ref[...].reshape(3 * channels, channels)
    projected = dot(weights, hbuf[...], 1, 1).astype(BF16)
    qkv[0:channels, :] = (projected[0:channels] * SCALE).astype(BF16)
    qkv[channels:, :] = projected[channels:]
    da[...] = dot(wp_ref[...], g_ref[...], 1, 1).astype(BF16)
    key = lax.broadcasted_iota(jnp.int32, (patch, patch), 0)
    query = lax.broadcasted_iota(jnp.int32, (patch, patch), 1)
    bias[...] = jnp.where(keep | (key == query), 0.0, NEGATIVE)

    def head(n, _):
        o = pl.multiple_of(n * HEAD, HEAD)
        qh = qkv[pl.ds(o, HEAD), :]
        kh = qkv[pl.ds(channels + o, HEAD), :]
        vh = qkv[pl.ds(2 * channels + o, HEAD), :]
        dah = da[pl.ds(o, HEAD), :]
        s = dot(kh, qh, 0, 0) + bias[...]
        e = jnp.exp(s - jnp.max(s, axis=0, keepdims=True))
        p = e * (1.0 / jnp.sum(e, axis=0, keepdims=True))
        pb = p.astype(BF16)
        a = dot(vh, pb)
        at[pl.ds(o, HEAD), :] = a.astype(BF16)
        delta = jnp.sum(dah.astype(F32) * a, axis=0, keepdims=True)
        dqkv[pl.ds(2 * channels + o, HEAD), :] = dot(dah, pb, 1, 1).astype(BF16)
        ds = (p * (dot(vh, dah, 0, 0) - delta)).astype(BF16)
        dqkv[pl.ds(o, HEAD), :] = (dot(kh, ds) * SCALE).astype(BF16)
        dqkv[pl.ds(channels + o, HEAD), :] = dot(qh, ds, 1, 1).astype(BF16)
        return 0

    lax.fori_loop(0, channels // HEAD, head, 0, unroll=2)

    a = at[...]
    dqkv_t = dqkv[...]
    x = x_ref[...].astype(F32)
    out = (keep.astype(F32) * (x + dot(a, wp_ref[...], 0, 0))).astype(BF16)
    dh = dot(dqkv_t, weights, 0, 0)
    xhat = (x - mu) * inv
    mean_dh = jnp.mean(dh, axis=1, keepdims=True)
    mean_dot = jnp.mean(dh * xhat, axis=1, keepdims=True)
    dx = (g_ref[...].astype(F32) + inv * (dh - mean_dh - xhat * mean_dot)).astype(BF16)
    grad_w = dot(dqkv_t, hbuf[...])
    grad_p = dot(a, g_ref[...])
    for r in range(reps):
        cols = slice(width * r, width * (r + 1))
        pay_ref[r, :, 0:width] = out[:, cols]
        pay_ref[r, :, width:] = dx[:, cols]
        for i in range(3):
            first = channels * i + width * r
            grad_ref[r, width * i : width * (i + 1), :] = grad_w[first : first + width]
        grad_ref[r, 3 * width :, :] = grad_p[cols]


def return_kernel(
    reps, group, pay_ref, grad_ref, order_ref,
    out_ref, gin_ref, gqkv_ref, gproj_ref,
    landed, core_out, core_in, rep_out, rep_in, z_out, z_in, x_all, total,
    pay_sems, core_sems, rep_sems, z_sems, x_sems, gather_sems, last_sems,
):
    me, rep = lax.axis_index("pts"), lax.axis_index("rep")
    member = lax.rem(me, group)
    base = me - member
    core = lax.rem(me, CORES)
    depth = group // CORES
    z = member // CORES
    row = me // group
    slots = landed.shape[0]
    patch = pay_ref.shape[1]
    block = patch // group
    half = core_in.shape[1]
    piece = half // depth
    partner = (me + 1 - 2 * core, rep)
    width = out_ref.shape[0]

    mates = [
        (lax.rem(rep + k, reps), lax.rem(member + n, group))
        for n in range(group) for k in range(reps) if k or n
    ]
    others_x = [lax.rem(row + k, reps) for k in range(1, reps)]
    peers_x = [(other * group + member, rep) for other in others_x]
    greet([(base + n, k) for k, n in mates] + peers_x)

    copies = []
    kept = pl.ds(pl.multiple_of(core * half, half), half)
    given = pl.ds(pl.multiple_of((1 - core) * half, half), half)
    core_out[...] = grad_ref[:, given, :].astype(BF16)
    to_core = send(core_out, core_in, core_sems.at[0], core_sems.at[1], partner)

    here = pl.ds(pl.multiple_of((rep * group + member) * block, block), block)
    for i, (k, n) in enumerate(mates):
        there = pl.ds(pl.multiple_of(n * block, block), block)
        copies.append(
            send(pay_ref.at[k, there, :], landed.at[here, :], pay_sems.at[0, i], pay_sems.at[1, i], (base + n, k))
        )
    landed[here, :] = pay_ref[rep, pl.ds(pl.multiple_of(member * block, block), block), :]

    to_core.wait()
    rep_out[...] = (grad_ref[:, kept, :] + core_in[...].astype(F32)).astype(BF16)
    to_rep = []
    for k in range(1, reps):
        other = lax.rem(rep + k, reps)
        to_rep.append(send(rep_out.at[other], rep_in.at[k - 1], rep_sems.at[0, k - 1], rep_sems.at[1, k - 1], (me, other)))
    partial = grad_ref[rep, kept, :] + core_in[rep].astype(F32)
    for copy in to_rep:
        copy.wait()
    for k in range(1, reps):
        partial = partial + rep_in[k - 1].astype(F32)
    z_out[...] = partial
    to_z = []
    for k in range(1, depth):
        other = lax.rem(z + k, depth)
        rows = pl.ds(pl.multiple_of(other * piece, piece), piece)
        to_z.append(
            send(z_out.at[rows, :], z_in.at[k - 1], z_sems.at[0, k - 1], z_sems.at[1, k - 1], (base + CORES * other + core, rep))
        )
    for copy in to_z:
        copy.wait()
    summed = z_out[pl.ds(pl.multiple_of(z * piece, piece), piece), :]
    for k in range(1, depth):
        summed = summed + z_in[k - 1]
    x_all[row] = summed
    to_x = [
        send(x_all.at[row], x_all.at[row], x_sems.at[0, k], x_sems.at[1, k], peer)
        for k, peer in enumerate(peers_x)
    ]
    for copy in to_x:
        copy.wait()
    summed = x_all[0]
    for k in range(1, reps):
        summed = summed + x_all[k]
    own = pl.ds(pl.multiple_of(core * half + z * piece, piece), piece)
    total[own, :] = summed
    to_all = [
        send(
            total.at[own, :], total.at[own, :], gather_sems.at[0, k - 1], gather_sems.at[1, k - 1],
            (base + CORES * lax.rem(z + k, depth) + core, rep),
        )
        for k in range(1, depth)
    ]
    for copy in to_all:
        copy.wait()
    last = send(total.at[kept, :], total.at[kept, :], last_sems.at[0], last_sems.at[1], partner)

    for copy in copies:
        copy.wait()
    target = column(order_ref[...])
    step = min(slots, 256)
    for first in range(0, slots, step):
        slot = lax.broadcasted_iota(jnp.int32, (slots, step), 1) + first
        place = jnp.where(target == slot, 1.0, 0.0).astype(BF16)
        back = dot(landed[...], place, 0, 0)
        out_ref[:, first : first + step] = back[0:width].astype(BF16)
        gin_ref[:, first : first + step] = back[width:]
    last.wait()
    for i in range(3):
        gqkv_ref[i] = total[width * i : width * (i + 1), :]
    gproj_ref[...] = total[3 * width :, :]


def shards(reps, group, points, counts, order, grad_out, w_qkv, w_proj):
    slots, channels = points.shape
    patch = slots // reps
    width = channels // reps
    depth = group // CORES
    half = 4 * width // CORES
    piece = half // depth
    order = order.reshape(1, slots)
    dma = pltpu.SemaphoreType.DMA
    x, g, w_all, wp_all = pl.pallas_call(
        functools.partial(gather_kernel, reps, group),
        out_shape=[
            jax.ShapeDtypeStruct((patch, channels), BF16),
            jax.ShapeDtypeStruct((patch, channels), BF16),
            jax.ShapeDtypeStruct((3, channels, channels), BF16),
            jax.ShapeDtypeStruct((channels, channels), BF16),
        ],
        in_specs=[VMEM, VMEM, VMEM, SMEM, VMEM, VMEM],
        out_specs=[VMEM] * 4,
        scratch_shapes=[
            pltpu.VMEM((patch, channels), BF16),
            pltpu.VMEM((patch, channels), BF16),
            dma((2, reps - 1)),
            dma((2, reps - 1)),
            dma((2, group - 1)),
            dma((2, group - 1)),
        ],
        compiler_params=pltpu.CompilerParams(
            collective_id=0, has_side_effects=True, vmem_limit_bytes=32 << 20
        ),
    )(points, grad_out, order, counts, w_qkv.transpose(0, 2, 1), w_proj)
    pay, grads = pl.pallas_call(
        functools.partial(attention_kernel, reps),
        out_shape=[
            jax.ShapeDtypeStruct((reps, patch, 2 * width), BF16),
            jax.ShapeDtypeStruct((reps, 4 * width, channels), F32),
        ],
        in_specs=[VMEM] * 4,
        out_specs=[VMEM] * 2,
        scratch_shapes=[
            pltpu.VMEM((3 * channels, patch), BF16),
            pltpu.VMEM((channels, patch), BF16),
            pltpu.VMEM((patch, patch), F32),
            pltpu.VMEM((channels, patch), BF16),
            pltpu.VMEM((3 * channels, patch), BF16),
            pltpu.VMEM((patch, channels), BF16),
        ],
        compiler_params=pltpu.CompilerParams(vmem_limit_bytes=48 << 20),
    )(x, g, w_all, wp_all)
    out, grad_input, grad_qkv, grad_proj = pl.pallas_call(
        functools.partial(return_kernel, reps, group),
        out_shape=[
            jax.ShapeDtypeStruct((width, slots), BF16),
            jax.ShapeDtypeStruct((width, slots), F32),
            jax.ShapeDtypeStruct((3, width, channels), F32),
            jax.ShapeDtypeStruct((width, channels), F32),
        ],
        in_specs=[VMEM] * 3,
        out_specs=[VMEM] * 4,
        scratch_shapes=[
            pltpu.VMEM((slots, 2 * width), BF16),
            pltpu.VMEM((reps, half, channels), BF16),
            pltpu.VMEM((reps, half, channels), BF16),
            pltpu.VMEM((reps, half, channels), BF16),
            pltpu.VMEM((reps - 1, half, channels), BF16),
            pltpu.VMEM((half, channels), F32),
            pltpu.VMEM((depth - 1, piece, channels), F32),
            pltpu.VMEM((reps, piece, channels), F32),
            pltpu.VMEM((4 * width, channels), F32),
            dma((2, group * reps - 1)),
            dma((2,)),
            dma((2, reps - 1)),
            dma((2, depth - 1)),
            dma((2, reps - 1)),
            dma((2, depth - 1)),
            dma((2,)),
        ],
        compiler_params=pltpu.CompilerParams(
            collective_id=1, has_side_effects=True, vmem_limit_bytes=48 << 20
        ),
    )(pay, grads, order)
    return out.T, grad_input.T, grad_qkv.transpose(0, 2, 1), grad_proj


def solution(mesh):
    reps = mesh.shape["rep"]
    group = mesh.shape["pts"] // reps
    return jax.shard_map(
        functools.partial(shards, reps, group),
        mesh=mesh,
        in_specs=(
            P("pts", None),
            P("pts"),
            P("pts"),
            P("pts", None),
            P(None, None, "rep"),
            P("rep", None),
        ),
        out_specs=(P("pts", "rep"), P("pts", "rep"), P(None, None, "rep"), P("rep", None)),
        check_vma=False,
    )
```

```python
import functools

import jax
import jax.numpy as jnp
from jax import lax
from jax.experimental import pallas as pl
from jax.experimental.pallas import tpu as pltpu
from jax.sharding import PartitionSpec as P

HEAD = 16
CORES = 2
SCALE = 0.25
EPS = 1e-05
NEGATIVE = -1e30
DEAD = 64.0
ALIVE_BELOW = 32.0
F32, BF16 = jnp.float32, jnp.bfloat16
MESH = pl.DeviceIdType.MESH
VMEM = pl.BlockSpec(memory_space=pltpu.VMEM)
SMEM = pl.BlockSpec(memory_space=pltpu.SMEM)


def dot(a, b, ca=1, cb=0):
    return lax.dot_general(a, b, (((ca,), (cb,)), ((), ())), preferred_element_type=F32)


def column(row):
    wide = jnp.broadcast_to(row.astype(F32), (8, row.shape[1]))
    return wide.T[:, 0:1].astype(jnp.int32)


def send(src, dst, send_sem, recv_sem, peer):
    copy = pltpu.make_async_remote_copy(
        src_ref=src, dst_ref=dst, send_sem=send_sem, recv_sem=recv_sem,
        device_id=peer, device_id_type=MESH,
    )
    copy.start()
    return copy


def pack(array, width, first, group):
    rows = array.shape[0]
    cut = array[:, first : first + width].reshape(group, 2, rows // group // 2, width)
    return jnp.concatenate([cut[:, 0].reshape(rows // 2, width), cut[:, 1].reshape(rows // 2, width)], axis=1)


def unpack(landed, place):
    width = landed.shape[1] // 2
    halves = landed.T
    return dot(jnp.concatenate([halves[:width], halves[width:]], axis=1), place)


def block_kernel(
    reps, group, points_hbm, grads_hbm, order_hbm, counts_ref, w_hbm, wp_hbm,
    out_ref, gin_ref, gqkv_ref, gproj_ref,
    points, grads, order, target, xs, gs, x_in, g_in, w_all, wp_all, place,
    qkv, da, bias, at, a_full, dqkv, hbuf, probs, recips,
    pay_out, pay_dx, landed_out, landed_dx,
    rep_out, rep_in, own, rs_out, rs_in, x_all, total,
    load_sems, w_sems, wp_sems, x_sems, g_sems, out_sems, dx_sems, rep_sems, rs_sems, row_sems, all_sems,
):
    me, rep = lax.axis_index("pts"), lax.axis_index("rep")
    member = lax.rem(me, group)
    base = me - member
    row = me // group
    slots, channels = points.shape
    patch = x_in.shape[0]
    block = patch // group
    width = channels // reps
    piece = 4 * width // group
    along = [lax.rem(member + k, group) for k in range(1, group)]
    beside = [(me, lax.rem(rep + k, reps)) for k in range(1, reps)]
    mates = [
        (lax.rem(rep + k, reps), lax.rem(member + n, group))
        for n in range(group) for k in range(reps) if k or n
    ]
    peers_x = [(lax.rem(row + k, reps) * group + member, rep) for k in range(1, reps)]

    mine = pl.ds(pl.multiple_of(rep * width, width), width)
    loads = []
    for i, (source, target_ref) in enumerate((
        (order_hbm, order), (points_hbm, points), (grads_hbm, grads),
        (w_hbm, w_all.at[:, mine, :]), (wp_hbm, wp_all.at[mine, :]),
    )):
        loads.append(pltpu.make_async_copy(source, target_ref, load_sems.at[i]))
        loads[-1].start()
    barrier = pltpu.get_barrier_semaphore()
    peers = [(base + n, k) for k, n in mates] + peers_x
    for peer in peers:
        pl.semaphore_signal(barrier, inc=1, device_id=peer, device_id_type=MESH)

    loads[0].wait()
    rows = column(order[:, pl.ds(pl.multiple_of(rep * patch, patch), patch)])
    live = rows < counts_ref[0]
    slot = lax.broadcasted_iota(jnp.int32, (patch, slots), 1)
    pick = jnp.where(rows == slot, 1.0, 0.0).astype(BF16)
    loads[1].wait()
    xs[...] = jnp.where(live, dot(pick, points[...]), DEAD).astype(BF16)
    pl.semaphore_wait(barrier, len(peers))

    sent, w_copies, x_copies, g_copies = [], [], [], []
    for k, peer in enumerate(beside):
        w_copies.append(send(w_hbm, w_all.at[:, mine, :], w_sems.at[0, k], w_sems.at[1, k], peer))
        w_copies.append(send(wp_hbm, wp_all.at[mine, :], wp_sems.at[0, k], wp_sems.at[1, k], peer))
    here = pl.ds(pl.multiple_of(member * block, block), block)

    def scatter(staged, landed, sems, copies):
        for k, other in enumerate(along):
            there = pl.ds(pl.multiple_of(other * block, block), block)
            copies.append(
                send(staged.at[there, :], landed.at[here, :], sems.at[0, k], sems.at[1, k], (base + other, rep))
            )
        landed[here, :] = staged[here, :]

    scatter(xs, x_in, x_sems, x_copies)
    loads[2].wait()
    gs[...] = jnp.where(live, dot(pick, grads[...]), 0.0).astype(BF16)
    scatter(gs, g_in, g_sems, g_copies)

    whole = column(order[...]).reshape(slots // block, 2, block // 2, 1)
    target[0 : slots // 2, :] = jnp.broadcast_to(whole[:, 0].reshape(slots // 2, 1), (slots // 2, 8))
    target[slots // 2 :, :] = jnp.broadcast_to(whole[:, 1].reshape(slots // 2, 1), (slots // 2, 8))
    chunk = 128

    def fill(c, _):
        rows = pl.ds(pl.multiple_of(c * chunk, chunk), chunk)
        arrival = lax.broadcasted_iota(jnp.int32, (chunk, slots), 1)
        place[rows, :] = jnp.where(target[rows, 0:1] == arrival, 1.0, 0.0).astype(BF16)
        return 0

    lax.fori_loop(0, slots // chunk, fill, 0)

    for copy in x_copies:
        copy.wait_recv()
    x = x_in[...].astype(F32)
    mu = jnp.mean(x, axis=1, keepdims=True)
    centered = x - mu
    inv = lax.rsqrt(jnp.mean(centered * centered, axis=1, keepdims=True) + EPS)
    hbuf[...] = (centered * inv).astype(BF16)
    keep = x[:, 0:1] < ALIVE_BELOW
    key = lax.broadcasted_iota(jnp.int32, (patch, patch), 0)
    query = lax.broadcasted_iota(jnp.int32, (patch, patch), 1)
    bias[...] = jnp.where(keep | (key == query), 0.0, NEGATIVE)
    loads[3].wait()
    loads[4].wait()
    for copy in w_copies:
        copy.wait_recv()
    projected = dot(w_all[...].reshape(3 * channels, channels), hbuf[...], 1, 1).astype(BF16)
    qkv[0:channels, :] = (projected[0:channels] * SCALE).astype(BF16)
    qkv[channels:, :] = projected[channels:]
    ones = jnp.ones((HEAD, patch), BF16)

    def heads(n):
        o = pl.multiple_of(n * HEAD, HEAD)
        return (
            pl.ds(o, HEAD), qkv[pl.ds(o, HEAD), :],
            qkv[pl.ds(channels + o, HEAD), :], qkv[pl.ds(2 * channels + o, HEAD), :],
        )

    def forward(n, _):
        rows, qh, kh, vh = heads(n)
        s = dot(kh, qh, 0, 0) + bias[...]
        e = jnp.exp(s - jnp.max(s, axis=0, keepdims=True)).astype(BF16)
        probs[n] = e
        mixed = dot(jnp.concatenate([vh, ones], axis=0), e)
        recip = 1.0 / mixed[HEAD : HEAD + 1]
        a = mixed[0:HEAD] * recip
        recips[pl.ds(n, 1), :] = recip
        a_full[rows, :] = a
        at[rows, :] = a.astype(BF16)
        return 0

    lax.fori_loop(0, channels // HEAD, forward, 0, unroll=4)
    x = x_in[...].astype(F32)
    out = (keep.astype(F32) * (x + dot(at[...], wp_all[...], 0, 0))).astype(BF16)
    back = pl.ds(pl.multiple_of((rep * group + member) * (block // 2), block // 2), block // 2)

    def give_back(array, pay, landed, sems):
        for r in range(reps):
            pay[r] = pack(array, width, width * r, group)
        copies = []
        for i, (k, n) in enumerate(mates):
            there = pl.ds(pl.multiple_of(n * (block // 2), block // 2), block // 2)
            copies.append(
                send(pay.at[k, there, :], landed.at[back, :], sems.at[0, i], sems.at[1, i], (base + n, k))
            )
        landed[back, :] = pay[rep, pl.ds(pl.multiple_of(member * (block // 2), block // 2), block // 2), :]
        return copies

    out_copies = give_back(out, pay_out, landed_out, out_sems)

    for copy in g_copies:
        copy.wait_recv()
    da[...] = dot(wp_all[...], g_in[...], 1, 1).astype(BF16)

    def backward(n, _):
        rows, qh, kh, vh = heads(n)
        dahf = da[rows, :].astype(F32) * recips[pl.ds(n, 1), :]
        dah = dahf.astype(BF16)
        delta = jnp.sum(dahf * a_full[rows, :], axis=0, keepdims=True)
        e = probs[n]
        o = pl.multiple_of(n * HEAD, HEAD)
        dqkv[pl.ds(2 * channels + o, HEAD), :] = dot(dah, e, 1, 1).astype(BF16)
        ds = (e.astype(F32) * (dot(vh, dah, 0, 0) - delta)).astype(BF16)
        dqkv[pl.ds(o, HEAD), :] = (dot(kh, ds) * SCALE).astype(BF16)
        dqkv[pl.ds(channels + o, HEAD), :] = dot(qh, ds, 1, 1).astype(BF16)
        return 0

    rep_copies = []
    per = width // HEAD
    for t in range(reps):
        part = lax.rem(rep + 1 + t, reps)
        lax.fori_loop(0, per, lambda i, _: backward(part * per + i, _), 0, unroll=4)
        first = pl.multiple_of(part * width, width)
        grown = [dqkv[pl.ds(channels * i + first, width), :] for i in range(3)]
        grad_w = dot(jnp.concatenate(grown, axis=0), hbuf[...])
        grad_p = dot(at[pl.ds(first, width), :], g_in[...])
        if t < reps - 1:
            rep_out[t, 0 : 3 * width, :] = grad_w.astype(BF16)
            rep_out[t, 3 * width :, :] = grad_p.astype(BF16)
            rep_copies.append(send(rep_out.at[t], rep_in.at[t], rep_sems.at[0, t], rep_sems.at[1, t], (me, part)))
        else:
            own[0 : 3 * width, :] = grad_w
            own[3 * width :, :] = grad_p

    dh = dot(dqkv[...], w_all[...].reshape(3 * channels, channels), 0, 0)
    xhat = (x_in[...].astype(F32) - mu) * inv
    mean_dh = jnp.mean(dh, axis=1, keepdims=True)
    mean_dot = jnp.mean(dh * xhat, axis=1, keepdims=True)
    dx = (g_in[...].astype(F32) + inv * (dh - mean_dh - xhat * mean_dot)).astype(BF16)
    dx_copies = give_back(dx, pay_dx, landed_dx, dx_sems)

    for copy in rep_copies:
        copy.wait_recv()
    partial = own[...]
    for t in range(reps - 1):
        partial = partial + rep_in[t].astype(F32)
    own[...] = partial
    rs_out[...] = partial.astype(BF16)
    rs_copies = []
    for k, other in enumerate(along):
        there = pl.ds(pl.multiple_of(other * piece, piece), piece)
        rs_copies.append(send(rs_out.at[there, :], rs_in.at[k], rs_sems.at[0, k], rs_sems.at[1, k], (base + other, rep)))
    for copy in out_copies:
        copy.wait_recv()
    out_ref[...] = unpack(landed_out[...], place[...]).astype(BF16)

    for copy in rs_copies:
        copy.wait_recv()
    mine = pl.ds(pl.multiple_of(member * piece, piece), piece)
    summed = own[mine, :]
    for k in range(group - 1):
        summed = summed + rs_in[k].astype(F32)
    x_all[row] = summed
    row_copies = [
        send(x_all.at[row], x_all.at[row], row_sems.at[0, k], row_sems.at[1, k], peer)
        for k, peer in enumerate(peers_x)
    ]
    for copy in row_copies:
        copy.wait_recv()
    summed = x_all[0]
    for k in range(1, reps):
        summed = summed + x_all[k]
    total[mine, :] = summed.astype(BF16)
    all_copies = [
        send(total.at[mine, :], total.at[mine, :], all_sems.at[0, k], all_sems.at[1, k], (base + other, rep))
        for k, other in enumerate(along)
    ]
    for copy in dx_copies:
        copy.wait_recv()
    gin_ref[...] = unpack(landed_dx[...], place[...])
    for copy in all_copies:
        copy.wait_recv()
    for i in range(3):
        gqkv_ref[i] = total[width * i : width * (i + 1), :].astype(F32)
    gproj_ref[...] = total[3 * width :, :].astype(F32)
    for copy in (
        w_copies + x_copies + g_copies + out_copies + dx_copies + rep_copies + rs_copies + row_copies + all_copies
    ):
        copy.wait_send()


def shards(reps, group, points, counts, order, grad_out, w_qkv, w_proj):
    slots, channels = points.shape
    patch = slots // reps
    width = channels // reps
    piece = 4 * width // group
    heads = channels // HEAD
    dma = pltpu.SemaphoreType.DMA
    vmem = pltpu.VMEM
    anywhere = pl.BlockSpec(memory_space=pl.ANY)
    out, grad_input, grad_qkv, grad_proj = pl.pallas_call(
        functools.partial(block_kernel, reps, group),
        out_shape=[
            jax.ShapeDtypeStruct((width, slots), BF16),
            jax.ShapeDtypeStruct((width, slots), F32),
            jax.ShapeDtypeStruct((3, width, channels), F32),
            jax.ShapeDtypeStruct((width, channels), F32),
        ],
        in_specs=[anywhere, anywhere, anywhere, SMEM, anywhere, anywhere],
        out_specs=[VMEM] * 4,
        scratch_shapes=[
            vmem((slots, channels), BF16),
            vmem((slots, channels), BF16),
            vmem((1, slots), jnp.int32),
            vmem((slots, 8), jnp.int32),
            vmem((patch, channels), BF16),
            vmem((patch, channels), BF16),
            vmem((patch, channels), BF16),
            vmem((patch, channels), BF16),
            vmem((3, channels, channels), BF16),
            vmem((channels, channels), BF16),
            vmem((slots, slots), BF16),
            vmem((3 * channels, patch), BF16),
            vmem((channels, patch), BF16),
            vmem((patch, patch), F32),
            vmem((channels, patch), BF16),
            vmem((channels, patch), F32),
            vmem((3 * channels, patch), BF16),
            vmem((patch, channels), BF16),
            vmem((heads, patch, patch), BF16),
            vmem((heads, patch), F32),
            vmem((reps, patch // 2, 2 * width), BF16),
            vmem((reps, patch // 2, 2 * width), BF16),
            vmem((slots // 2, 2 * width), BF16),
            vmem((slots // 2, 2 * width), BF16),
            vmem((reps - 1, 4 * width, channels), BF16),
            vmem((reps - 1, 4 * width, channels), BF16),
            vmem((4 * width, channels), F32),
            vmem((4 * width, channels), BF16),
            vmem((group - 1, piece, channels), BF16),
            vmem((reps, piece, channels), F32),
            vmem((4 * width, channels), BF16),
            dma((5,)),
            dma((2, reps - 1)),
            dma((2, reps - 1)),
            dma((2, group - 1)),
            dma((2, group - 1)),
            dma((2, group * reps - 1)),
            dma((2, group * reps - 1)),
            dma((2, reps - 1)),
            dma((2, group - 1)),
            dma((2, reps - 1)),
            dma((2, group - 1)),
        ],
        compiler_params=pltpu.CompilerParams(
            collective_id=0, has_side_effects=True, vmem_limit_bytes=56 << 20
        ),
    )(points, grad_out, order.reshape(1, slots), counts, w_qkv.transpose(0, 2, 1), w_proj)
    return out.T, grad_input.T, grad_qkv.transpose(0, 2, 1), grad_proj


def solution(mesh):
    reps = mesh.shape["rep"]
    group = mesh.shape["pts"] // reps
    return jax.shard_map(
        functools.partial(shards, reps, group),
        mesh=mesh,
        in_specs=(
            P("pts", None),
            P("pts"),
            P("pts"),
            P("pts", None),
            P(None, None, "rep"),
            P("rep", None),
        ),
        out_specs=(P("pts", "rep"), P("pts", "rep"), P(None, None, "rep"), P("rep", None)),
        check_vma=False,
    )
```

```python
import functools

import jax
import jax.numpy as jnp
from jax import lax
from jax.experimental import pallas as pl
from jax.experimental.pallas import tpu as pltpu
from jax.sharding import PartitionSpec as P

HEAD = 16
CORES = 2
SCALE = 0.25
EPS = 1e-05
NEGATIVE = -1e30
DEAD = 64.0
ALIVE_BELOW = 32.0
F32, BF16 = jnp.float32, jnp.bfloat16
MESH = pl.DeviceIdType.MESH
VMEM = pl.BlockSpec(memory_space=pltpu.VMEM)
SMEM = pl.BlockSpec(memory_space=pltpu.SMEM)


def dot(a, b, ca=1, cb=0):
    return lax.dot_general(a, b, (((ca,), (cb,)), ((), ())), preferred_element_type=F32)


def column(row):
    wide = jnp.broadcast_to(row.astype(F32), (8, row.shape[1]))
    return wide.T[:, 0:1].astype(jnp.int32)


def send(src, dst, send_sem, recv_sem, peer):
    copy = pltpu.make_async_remote_copy(
        src_ref=src, dst_ref=dst, send_sem=send_sem, recv_sem=recv_sem,
        device_id=peer, device_id_type=MESH,
    )
    copy.start()
    return copy


def far_first(n):
    return sorted(range(n), key=lambda k: -min(k, n - k))


def pack(array, width, first, group):
    rows = array.shape[0]
    cut = array[:, first : first + width].reshape(group, 2, rows // group // 2, width)
    return jnp.concatenate([cut[:, 0].reshape(rows // 2, width), cut[:, 1].reshape(rows // 2, width)], axis=1)


def unpack(landed, place):
    width = landed.shape[1] // 2
    halves = landed.T
    return dot(jnp.concatenate([halves[:width], halves[width:]], axis=1), place)


def block_kernel(
    reps, group, points_hbm, grads_hbm, order_hbm, counts_ref, w_hbm, wp_hbm,
    out_ref, gin_ref, gqkv_ref, gproj_ref,
    points, grads, order, target, xs, gs, x_in, g_in, w_all, wp_all, place,
    qkv, da, bias, at, a_full, dqkv, hbuf, probs, recips,
    pay_out, pay_dx, landed_out, landed_dx,
    rep_out, rep_in, core_out, core_in, own, z_out, z_in, x_all, total,
    load_sems, w_sems, wp_sems, x_sems, g_sems, out_sems, dx_sems, rep_sems,
    core_sems, z_sems, row_sems, all_sems, last_sems,
):
    me, rep = lax.axis_index("pts"), lax.axis_index("rep")
    member = lax.rem(me, group)
    base = me - member
    row = me // group
    slots, channels = points.shape
    patch = x_in.shape[0]
    block = patch // group
    width = channels // reps
    half = 2 * width
    depth = group // CORES
    piece = half // depth
    z, core = member // CORES, lax.rem(member, CORES)
    partner = (base + CORES * z + 1 - core, rep)

    def moved(dz, dc):
        return CORES * lax.rem(z + dz, depth) + lax.rem(core + dc, CORES)

    steps = [(dz, dc) for dz in far_first(depth) for dc in range(CORES)]
    along = [moved(dz, dc) for dz, dc in steps if dz or dc]
    along_z = [lax.rem(z + dz, depth) for dz in far_first(depth) if dz]
    beside = [(me, lax.rem(rep + k, reps)) for k in far_first(reps) if k]
    mates = [
        (lax.rem(rep + k, reps), moved(dz, dc))
        for dz, dc in steps for k in far_first(reps) if k or dz or dc
    ]
    peers_x = [(lax.rem(row + k, reps) * group + member, rep) for k in far_first(reps) if k]

    mine = pl.ds(pl.multiple_of(rep * width, width), width)
    loads = []
    for i, (source, target_ref) in enumerate((
        (order_hbm, order), (points_hbm, points), (grads_hbm, grads),
        (w_hbm, w_all.at[:, mine, :]), (wp_hbm, wp_all.at[mine, :]),
    )):
        loads.append(pltpu.make_async_copy(source, target_ref, load_sems.at[i]))
        loads[-1].start()
    barrier = pltpu.get_barrier_semaphore()
    peers = [(base + n, rep) for n in along] + beside + peers_x
    for peer in peers:
        pl.semaphore_signal(barrier, inc=1, device_id=peer, device_id_type=MESH)

    loads[0].wait()
    rows = column(order[:, pl.ds(pl.multiple_of(rep * patch, patch), patch)])
    live = rows < counts_ref[0]
    slot = lax.broadcasted_iota(jnp.int32, (patch, slots), 1)
    pick = jnp.where(rows == slot, 1.0, 0.0).astype(BF16)
    loads[1].wait()
    xs[...] = jnp.where(live, dot(pick, points[...]), DEAD).astype(BF16)
    pl.semaphore_wait(barrier, len(peers))

    sent, w_copies, x_copies, g_copies = [], [], [], []
    for k, peer in enumerate(beside):
        w_copies.append(send(w_hbm, w_all.at[:, mine, :], w_sems.at[0, k], w_sems.at[1, k], peer))
        w_copies.append(send(wp_hbm, wp_all.at[mine, :], wp_sems.at[0, k], wp_sems.at[1, k], peer))
    here = pl.ds(pl.multiple_of(member * block, block), block)

    def scatter(staged, landed, sems, copies):
        for k, other in enumerate(along):
            there = pl.ds(pl.multiple_of(other * block, block), block)
            copies.append(
                send(staged.at[there, :], landed.at[here, :], sems.at[0, k], sems.at[1, k], (base + other, rep))
            )
        landed[here, :] = staged[here, :]

    scatter(xs, x_in, x_sems, x_copies)
    loads[2].wait()
    gs[...] = jnp.where(live, dot(pick, grads[...]), 0.0).astype(BF16)

    whole = column(order[...]).reshape(slots // block, 2, block // 2, 1)
    target[0 : slots // 2, :] = jnp.broadcast_to(whole[:, 0].reshape(slots // 2, 1), (slots // 2, 8))
    target[slots // 2 :, :] = jnp.broadcast_to(whole[:, 1].reshape(slots // 2, 1), (slots // 2, 8))
    chunk = 128

    def fill(c, _):
        rows = pl.ds(pl.multiple_of(c * chunk, chunk), chunk)
        arrival = lax.broadcasted_iota(jnp.int32, (chunk, slots), 1)
        place[rows, :] = jnp.where(target[rows, 0:1] == arrival, 1.0, 0.0).astype(BF16)
        return 0

    lax.fori_loop(0, slots // chunk, fill, 0)

    for copy in x_copies:
        copy.wait_recv()
    scatter(gs, g_in, g_sems, g_copies)
    x = x_in[...].astype(F32)
    mu = jnp.mean(x, axis=1, keepdims=True)
    centered = x - mu
    inv = lax.rsqrt(jnp.mean(centered * centered, axis=1, keepdims=True) + EPS)
    hbuf[...] = (centered * inv).astype(BF16)
    keep = x[:, 0:1] < ALIVE_BELOW
    key = lax.broadcasted_iota(jnp.int32, (patch, patch), 0)
    query = lax.broadcasted_iota(jnp.int32, (patch, patch), 1)
    bias[...] = jnp.where(keep | (key == query), 0.0, NEGATIVE)
    loads[3].wait()
    loads[4].wait()
    for copy in w_copies:
        copy.wait_recv()
    projected = dot(w_all[...].reshape(3 * channels, channels), hbuf[...], 1, 1).astype(BF16)
    qkv[0:channels, :] = (projected[0:channels] * SCALE).astype(BF16)
    qkv[channels:, :] = projected[channels:]
    ones = jnp.ones((HEAD, patch), BF16)

    def heads(n):
        o = pl.multiple_of(n * HEAD, HEAD)
        return (
            pl.ds(o, HEAD), qkv[pl.ds(o, HEAD), :],
            qkv[pl.ds(channels + o, HEAD), :], qkv[pl.ds(2 * channels + o, HEAD), :],
        )

    def forward(n, _):
        rows, qh, kh, vh = heads(n)
        s = dot(kh, qh, 0, 0) + bias[...]
        e = jnp.exp(s - jnp.max(s, axis=0, keepdims=True)).astype(BF16)
        probs[n] = e
        mixed = dot(jnp.concatenate([vh, ones], axis=0), e)
        recip = 1.0 / mixed[HEAD : HEAD + 1]
        a = mixed[0:HEAD] * recip
        recips[pl.ds(n, 1), :] = recip
        a_full[rows, :] = a
        at[rows, :] = a.astype(BF16)
        return 0

    lax.fori_loop(0, channels // HEAD, forward, 0, unroll=4)
    x = x_in[...].astype(F32)
    out = (keep.astype(F32) * (x + dot(at[...], wp_all[...], 0, 0))).astype(BF16)
    back = pl.ds(pl.multiple_of((rep * group + member) * (block // 2), block // 2), block // 2)

    def give_back(array, pay, landed, sems):
        for r in range(reps):
            pay[r] = pack(array, width, width * r, group)
        copies = []
        for i, (k, n) in enumerate(mates):
            there = pl.ds(pl.multiple_of(n * (block // 2), block // 2), block // 2)
            copies.append(
                send(pay.at[k, there, :], landed.at[back, :], sems.at[0, i], sems.at[1, i], (base + n, k))
            )
        landed[back, :] = pay[rep, pl.ds(pl.multiple_of(member * (block // 2), block // 2), block // 2), :]
        return copies

    out_copies = give_back(out, pay_out, landed_out, out_sems)

    for copy in g_copies:
        copy.wait_recv()
    da[...] = dot(wp_all[...], g_in[...], 1, 1).astype(BF16)

    def backward(n, _):
        rows, qh, kh, vh = heads(n)
        dahf = da[rows, :].astype(F32) * recips[pl.ds(n, 1), :]
        dah = dahf.astype(BF16)
        delta = jnp.sum(dahf * a_full[rows, :], axis=0, keepdims=True)
        e = probs[n]
        o = pl.multiple_of(n * HEAD, HEAD)
        dqkv[pl.ds(2 * channels + o, HEAD), :] = dot(dah, e, 1, 1).astype(BF16)
        ds = (e.astype(F32) * (dot(vh, dah, 0, 0) - delta)).astype(BF16)
        dqkv[pl.ds(o, HEAD), :] = (dot(kh, ds) * SCALE).astype(BF16)
        dqkv[pl.ds(channels + o, HEAD), :] = dot(qh, ds, 1, 1).astype(BF16)
        return 0

    rep_copies = []
    per = width // HEAD
    for t in range(reps):
        part = lax.rem(rep + 1 + t, reps)
        lax.fori_loop(0, per, lambda i, _: backward(part * per + i, _), 0, unroll=4)
        first = pl.multiple_of(part * width, width)
        grown = [dqkv[pl.ds(channels * i + first, width), :] for i in range(3)]
        grad_w = dot(jnp.concatenate(grown, axis=0), hbuf[...])
        grad_p = dot(at[pl.ds(first, width), :], g_in[...])
        if t < reps - 1:
            rep_out[t, 0 : 3 * width, :] = grad_w.astype(BF16)
            rep_out[t, 3 * width :, :] = grad_p.astype(BF16)
            rep_copies.append(send(rep_out.at[t], rep_in.at[t], rep_sems.at[0, t], rep_sems.at[1, t], (me, part)))
        else:
            own[0 : 3 * width, :] = grad_w
            own[3 * width :, :] = grad_p

    for copy in rep_copies:
        copy.wait_recv()
    partial = own[...]
    for t in range(reps - 1):
        partial = partial + rep_in[t].astype(F32)
    own[...] = partial
    kept = pl.ds(pl.multiple_of(core * half, half), half)
    core_out[...] = own[pl.ds(pl.multiple_of((1 - core) * half, half), half), :].astype(BF16)
    to_core = send(core_out, core_in, core_sems.at[0], core_sems.at[1], partner)

    dh = dot(dqkv[...], w_all[...].reshape(3 * channels, channels), 0, 0)
    xhat = (x_in[...].astype(F32) - mu) * inv
    mean_dh = jnp.mean(dh, axis=1, keepdims=True)
    mean_dot = jnp.mean(dh * xhat, axis=1, keepdims=True)
    dx = (g_in[...].astype(F32) + inv * (dh - mean_dh - xhat * mean_dot)).astype(BF16)

    to_core.wait_recv()
    partial = own[kept, :] + core_in[...].astype(F32)
    own[0:half, :] = partial
    z_out[...] = partial.astype(BF16)
    z_copies = []
    for k, other in enumerate(along_z):
        there = pl.ds(pl.multiple_of(other * piece, piece), piece)
        z_copies.append(
            send(z_out.at[there, :], z_in.at[k], z_sems.at[0, k], z_sems.at[1, k], (base + CORES * other + core, rep))
        )
    dx_copies = give_back(dx, pay_dx, landed_dx, dx_sems)

    for copy in z_copies:
        copy.wait_recv()
    summed = own[pl.ds(pl.multiple_of(z * piece, piece), piece), :]
    for k in range(depth - 1):
        summed = summed + z_in[k].astype(F32)
    x_all[row] = summed
    row_copies = [
        send(x_all.at[row], x_all.at[row], row_sems.at[0, k], row_sems.at[1, k], peer)
        for k, peer in enumerate(peers_x)
    ]
    for copy in out_copies:
        copy.wait_recv()
    out_ref[...] = unpack(landed_out[...], place[...]).astype(BF16)
    for copy in row_copies:
        copy.wait_recv()
    summed = x_all[0]
    for k in range(1, reps):
        summed = summed + x_all[k]
    done = pl.ds(pl.multiple_of(core * half + z * piece, piece), piece)
    total[done, :] = summed.astype(BF16)
    all_copies = [
        send(
            total.at[done, :], total.at[done, :], all_sems.at[0, k], all_sems.at[1, k],
            (base + CORES * other + core, rep),
        )
        for k, other in enumerate(along_z)
    ]
    for copy in dx_copies:
        copy.wait_recv()
    gin_ref[...] = unpack(landed_dx[...], place[...])
    for copy in all_copies:
        copy.wait_recv()
    last = send(total.at[kept, :], total.at[kept, :], last_sems.at[0], last_sems.at[1], partner)
    last.wait_recv()
    for i in range(3):
        gqkv_ref[i] = total[width * i : width * (i + 1), :].astype(F32)
    gproj_ref[...] = total[3 * width :, :].astype(F32)
    for copy in (
        w_copies + x_copies + g_copies + out_copies + dx_copies + rep_copies
        + [to_core] + z_copies + row_copies + all_copies + [last]
    ):
        copy.wait_send()


def copy_kernel(*refs):
    count = len(refs) // 2
    sources, targets, sems = refs[:count], refs[count : 2 * count], refs[2 * count]
    copies = [pltpu.make_async_copy(a, b, sems.at[i]) for i, (a, b) in enumerate(zip(sources, targets))]
    for copy in copies:
        copy.start()
    for copy in copies:
        copy.wait()


def copy_out(arrays):
    return pl.pallas_call(
        copy_kernel,
        out_shape=[jax.ShapeDtypeStruct(a.shape, a.dtype) for a in arrays],
        in_specs=[pl.BlockSpec(memory_space=pl.ANY)] * len(arrays),
        out_specs=[pl.BlockSpec(memory_space=pl.ANY)] * len(arrays),
        scratch_shapes=[pltpu.SemaphoreType.DMA((len(arrays),))],
        compiler_params=pltpu.CompilerParams(vmem_limit_bytes=1 << 20),
    )(*arrays)


def shards(reps, group, points, counts, order, grad_out, w_qkv, w_proj):
    slots, channels = points.shape
    patch = slots // reps
    width = channels // reps
    half = 2 * width
    piece = half // (group // CORES)
    heads = channels // HEAD
    dma = pltpu.SemaphoreType.DMA
    vmem = pltpu.VMEM
    anywhere = pl.BlockSpec(memory_space=pl.ANY)
    results = pl.pallas_call(
        functools.partial(block_kernel, reps, group),
        out_shape=[
            jax.ShapeDtypeStruct((width, slots), BF16),
            jax.ShapeDtypeStruct((width, slots), F32),
            jax.ShapeDtypeStruct((3, width, channels), F32),
            jax.ShapeDtypeStruct((width, channels), F32),
        ],
        in_specs=[anywhere, anywhere, anywhere, SMEM, anywhere, anywhere],
        out_specs=[VMEM] * 4,
        scratch_shapes=[
            vmem((slots, channels), BF16),
            vmem((slots, channels), BF16),
            vmem((1, slots), jnp.int32),
            vmem((slots, 8), jnp.int32),
            vmem((patch, channels), BF16),
            vmem((patch, channels), BF16),
            vmem((patch, channels), BF16),
            vmem((patch, channels), BF16),
            vmem((3, channels, channels), BF16),
            vmem((channels, channels), BF16),
            vmem((slots, slots), BF16),
            vmem((3 * channels, patch), BF16),
            vmem((channels, patch), BF16),
            vmem((patch, patch), F32),
            vmem((channels, patch), BF16),
            vmem((channels, patch), F32),
            vmem((3 * channels, patch), BF16),
            vmem((patch, channels), BF16),
            vmem((heads, patch, patch), BF16),
            vmem((heads, patch), F32),
            vmem((reps, patch // 2, 2 * width), BF16),
            vmem((reps, patch // 2, 2 * width), BF16),
            vmem((slots // 2, 2 * width), BF16),
            vmem((slots // 2, 2 * width), BF16),
            vmem((reps - 1, 4 * width, channels), BF16),
            vmem((reps - 1, 4 * width, channels), BF16),
            vmem((half, channels), BF16),
            vmem((half, channels), BF16),
            vmem((4 * width, channels), F32),
            vmem((half, channels), BF16),
            vmem((group // CORES - 1, piece, channels), BF16),
            vmem((reps, piece, channels), F32),
            vmem((4 * width, channels), BF16),
            dma((5,)),
            dma((2, reps - 1)),
            dma((2, reps - 1)),
            dma((2, group - 1)),
            dma((2, group - 1)),
            dma((2, group * reps - 1)),
            dma((2, group * reps - 1)),
            dma((2, reps - 1)),
            dma((2,)),
            dma((2, group // CORES - 1)),
            dma((2, reps - 1)),
            dma((2, group // CORES - 1)),
            dma((2,)),
        ],
        compiler_params=pltpu.CompilerParams(
            collective_id=0, has_side_effects=True, vmem_limit_bytes=52 << 20
        ),
    )(points, grad_out, order.reshape(1, slots), counts, w_qkv.transpose(0, 2, 1), w_proj)
    out, grad_input, grad_qkv, grad_proj = copy_out(results)
    return out.T, grad_input.T, grad_qkv.transpose(0, 2, 1), grad_proj


def solution(mesh):
    reps = mesh.shape["rep"]
    group = mesh.shape["pts"] // reps
    return jax.shard_map(
        functools.partial(shards, reps, group),
        mesh=mesh,
        in_specs=(
            P("pts", None),
            P("pts"),
            P("pts"),
            P("pts", None),
            P(None, None, "rep"),
            P("rep", None),
        ),
        out_specs=(P("pts", "rep"), P("pts", "rep"), P(None, None, "rep"), P("rep", None)),
        check_vma=False,
    )
```

```python
import functools

import jax
import jax.numpy as jnp
from jax import lax
from jax.experimental import pallas as pl
from jax.experimental.pallas import tpu as pltpu
from jax.sharding import PartitionSpec as P

HEAD = 16
CORES = 2
SCALE = 0.25
EPS = 1e-05
NEGATIVE = -1e30
DEAD = 64.0
ALIVE_BELOW = 32.0
F32, BF16 = jnp.float32, jnp.bfloat16
MESH = pl.DeviceIdType.MESH
VMEM = pl.BlockSpec(memory_space=pltpu.VMEM)
SMEM = pl.BlockSpec(memory_space=pltpu.SMEM)


def dot(a, b, ca=1, cb=0):
    return lax.dot_general(a, b, (((ca,), (cb,)), ((), ())), preferred_element_type=F32)


def column(row):
    wide = jnp.broadcast_to(row.astype(F32), (8, row.shape[1]))
    return wide.T[:, 0:1].astype(jnp.int32)


def send(src, dst, send_sem, recv_sem, peer):
    copy = pltpu.make_async_remote_copy(
        src_ref=src, dst_ref=dst, send_sem=send_sem, recv_sem=recv_sem,
        device_id=peer, device_id_type=MESH,
    )
    copy.start()
    return copy


def far_first(n):
    return sorted(range(n), key=lambda k: -min(k, n - k))


def pack(array, width, first, group):
    rows = array.shape[0]
    cut = array[:, first : first + width].reshape(group, 2, rows // group // 2, width)
    return jnp.concatenate([cut[:, 0].reshape(rows // 2, width), cut[:, 1].reshape(rows // 2, width)], axis=1)


def unpack(landed, place):
    width = landed.shape[1] // 2
    halves = landed.T
    return dot(jnp.concatenate([halves[:width], halves[width:]], axis=1), place)


def unpack_all(landed, place, depth):
    width = landed.shape[1] // 2
    halves = landed[...].T
    lines = landed.shape[0] // depth
    cuts = [
        halves[width * h : width * (h + 1), lines * zz : lines * (zz + 1)] for zz in range(depth) for h in range(2)
    ]
    return dot(jnp.concatenate(cuts, axis=1), place[...])


def block_kernel(
    reps, group, points_hbm, grads_hbm, order_hbm, counts_ref, w_hbm, wp_hbm,
    out_ref, gin_ref, gqkv_ref, gproj_ref,
    points, grads, order, target, xs, gs, x_in, g_in, w_all, wp_all, place,
    qkv, da, bias, scores, at, a_full, dqkv, hbuf, probs, recips,
    pay_out, pay_dx, landed_out, landed_dx,
    rep_out, rep_in, core_out, core_in, own, z_out, z_in, x_all, total,
    load_sems, w_sems, wp_sems, x_sems, g_sems, out_sems, dx_sems, rep_sems,
    core_sems, z_sems, row_sems, all_sems, last_sems,
):
    me, rep = lax.axis_index("pts"), lax.axis_index("rep")
    member = lax.rem(me, group)
    base = me - member
    row = me // group
    slots, channels = points.shape
    patch = x_in.shape[0]
    block = patch // group
    width = channels // reps
    half = 2 * width
    depth = group // CORES
    piece = half // depth
    z, core = member // CORES, lax.rem(member, CORES)
    partner = (base + CORES * z + 1 - core, rep)

    def moved(dz, dc):
        return CORES * lax.rem(z + dz, depth) + lax.rem(core + dc, CORES)

    steps = [(dz, dc) for dz in far_first(depth) for dc in range(CORES)]
    along = [moved(dz, dc) for dz, dc in steps if dz or dc]
    along_z = [lax.rem(z + dz, depth) for dz in far_first(depth) if dz]
    beside = [(me, lax.rem(rep + k, reps)) for k in far_first(reps) if k]
    mates = [
        (lax.rem(rep + k, reps), moved(dz, dc))
        for dz, dc in steps for k in far_first(reps) if k or dz or dc
    ]
    ends = [step for step in steps for k in far_first(reps) if k or step != (0, 0)]
    peers_x = [(lax.rem(row + k, reps) * group + member, rep) for k in far_first(reps) if k]

    mine = pl.ds(pl.multiple_of(rep * width, width), width)
    loads = []
    for i, (source, target_ref) in enumerate((
        (order_hbm, order), (points_hbm, points), (grads_hbm, grads),
        (w_hbm, w_all.at[:, mine, :]), (wp_hbm, wp_all.at[mine, :]),
    )):
        loads.append(pltpu.make_async_copy(source, target_ref, load_sems.at[i]))
        loads[-1].start()
    barrier = pltpu.get_barrier_semaphore()
    peers = [(base + n, rep) for n in along] + beside + peers_x
    for peer in peers:
        pl.semaphore_signal(barrier, inc=1, device_id=peer, device_id_type=MESH)

    loads[0].wait()
    rows = column(order[:, pl.ds(pl.multiple_of(rep * patch, patch), patch)])
    live = rows < counts_ref[0]
    slot = lax.broadcasted_iota(jnp.int32, (patch, slots), 1)
    pick = jnp.where(rows == slot, 1.0, 0.0).astype(BF16)
    loads[1].wait()
    xs[...] = jnp.where(live, dot(pick, points[...]), DEAD).astype(BF16)
    pl.semaphore_wait(barrier, len(peers))

    sent, w_copies, x_copies, g_copies = [], [], [], []
    for k, peer in enumerate(beside):
        w_copies.append(send(w_hbm, w_all.at[:, mine, :], w_sems.at[0, k], w_sems.at[1, k], peer))
        w_copies.append(send(wp_hbm, wp_all.at[mine, :], wp_sems.at[0, k], wp_sems.at[1, k], peer))
    here = pl.ds(pl.multiple_of(member * block, block), block)

    def scatter(staged, landed, sems, copies):
        for k, other in enumerate(along):
            there = pl.ds(pl.multiple_of(other * block, block), block)
            copies.append(
                send(staged.at[there, :], landed.at[here, :], sems.at[0, k], sems.at[1, k], (base + other, rep))
            )
        landed[here, :] = staged[here, :]

    scatter(xs, x_in, x_sems, x_copies)
    loads[2].wait()
    gs[...] = jnp.where(live, dot(pick, grads[...]), 0.0).astype(BF16)

    whole = column(order[...])
    small = block // 2
    first = 0
    for zz in range(depth):
        for hh in range(2):
            for cc in range(CORES):
                for k in range(reps):
                    start = ((k * depth + zz) * CORES + cc) * block + hh * small
                    target[first : first + small, :] = jnp.broadcast_to(whole[start : start + small], (small, 8))
                    first += small
    chunk = 128

    def fill(c, _):
        rows = pl.ds(pl.multiple_of(c * chunk, chunk), chunk)
        arrival = lax.broadcasted_iota(jnp.int32, (chunk, slots), 1)
        place[rows, :] = jnp.where(target[rows, 0:1] == arrival, 1.0, 0.0).astype(BF16)
        return 0

    lax.fori_loop(0, slots // chunk, fill, 0)

    for copy in x_copies:
        copy.wait_recv()
    scatter(gs, g_in, g_sems, g_copies)
    x = x_in[...].astype(F32)
    mu = jnp.mean(x, axis=1, keepdims=True)
    centered = x - mu
    inv = lax.rsqrt(jnp.mean(centered * centered, axis=1, keepdims=True) + EPS)
    hbuf[...] = (centered * inv).astype(BF16)
    keep = x[:, 0:1] < ALIVE_BELOW
    key = lax.broadcasted_iota(jnp.int32, (patch, patch), 0)
    query = lax.broadcasted_iota(jnp.int32, (patch, patch), 1)
    bias[...] = jnp.where(keep | (key == query), 0.0, NEGATIVE)
    loads[3].wait()
    loads[4].wait()
    for copy in w_copies:
        copy.wait_recv()
    projected = dot(w_all[...].reshape(3 * channels, channels), hbuf[...], 1, 1).astype(BF16)
    qkv[0:channels, :] = (projected[0:channels] * SCALE).astype(BF16)
    qkv[channels:, :] = projected[channels:]
    ones = jnp.ones((HEAD, patch), BF16)

    def heads(n):
        o = pl.multiple_of(n * HEAD, HEAD)
        return (
            pl.ds(o, HEAD), qkv[pl.ds(o, HEAD), :],
            qkv[pl.ds(channels + o, HEAD), :], qkv[pl.ds(2 * channels + o, HEAD), :],
        )

    def score(n):
        _, qh, kh, _ = heads(n)
        return dot(kh, qh, 0, 0) + bias[...]

    def mix(n, s):
        rows, _, _, vh = heads(n)
        e = jnp.exp(s - jnp.max(s, axis=0, keepdims=True)).astype(BF16)
        probs[n] = e
        mixed = dot(jnp.concatenate([vh, ones], axis=0), e)
        recip = 1.0 / mixed[HEAD : HEAD + 1]
        a = mixed[0:HEAD] * recip
        recips[pl.ds(n, 1), :] = recip
        a_full[rows, :] = a
        at[rows, :] = a.astype(BF16)

    count = channels // HEAD
    unrolled = 8

    def forward(i, _):
        for j in range(unrolled):
            n = i * unrolled + j
            follower = lax.rem(n + 1, count) if j == unrolled - 1 else n + 1
            scores[(j + 1) % 2] = score(follower)
            mix(n, scores[j % 2])
        return 0

    scores[0] = score(0)
    lax.fori_loop(0, count // unrolled, forward, 0)
    x = x_in[...].astype(F32)
    out = (keep.astype(F32) * (x + dot(at[...], wp_all[...], 0, 0))).astype(BF16)
    back = pl.ds(pl.multiple_of((member * reps + rep) * small, small), small)

    def stage(array, pay, landed):
        for r in range(reps):
            pay[r] = pack(array, width, width * r, group)
        landed[back, :] = pay[rep, pl.ds(pl.multiple_of(member * small, small), small), :]

    def give_back(pay, landed, sems, which):
        copies = []
        for i in which:
            k, n = mates[i]
            there = pl.ds(pl.multiple_of(n * small, small), small)
            copies.append(
                send(pay.at[k, there, :], landed.at[back, :], sems.at[0, i], sems.at[1, i], (base + n, k))
            )
        return copies

    stage(out, pay_out, landed_out)
    out_copies = give_back(pay_out, landed_out, out_sems, range(len(mates)))

    for copy in g_copies:
        copy.wait_recv()
    da[...] = dot(wp_all[...], g_in[...], 1, 1).astype(BF16)

    def backward(n):
        rows, qh, kh, vh = heads(n)
        dahf = da[rows, :].astype(F32) * recips[pl.ds(n, 1), :]
        dah = dahf.astype(BF16)
        delta = jnp.sum(dahf * a_full[rows, :], axis=0, keepdims=True)
        e = probs[n]
        o = pl.multiple_of(n * HEAD, HEAD)
        dp = dot(vh, dah, 0, 0)
        dqkv[pl.ds(2 * channels + o, HEAD), :] = dot(dah, e, 1, 1).astype(BF16)
        ds = (e.astype(F32) * (dp - delta)).astype(BF16)
        dqkv[pl.ds(o, HEAD), :] = (dot(kh, ds) * SCALE).astype(BF16)
        dqkv[pl.ds(channels + o, HEAD), :] = dot(qh, ds, 1, 1).astype(BF16)

    rep_copies = []
    per = width // HEAD
    for t in range(reps):
        part = lax.rem(rep + 1 + t, reps)
        for i in range(per):
            backward(part * per + i)
        first = pl.multiple_of(part * width, width)
        grown = [dqkv[pl.ds(channels * i + first, width), :] for i in range(3)]
        grad_w = dot(jnp.concatenate(grown, axis=0), hbuf[...])
        grad_p = dot(at[pl.ds(first, width), :], g_in[...])
        if t < reps - 1:
            rep_out[t, 0 : 3 * width, :] = grad_w.astype(BF16)
            rep_out[t, 3 * width :, :] = grad_p.astype(BF16)
            rep_copies.append(send(rep_out.at[t], rep_in.at[t], rep_sems.at[0, t], rep_sems.at[1, t], (me, part)))
        else:
            own[0 : 3 * width, :] = grad_w
            own[3 * width :, :] = grad_p

    dh = dot(dqkv[...], w_all[...].reshape(3 * channels, channels), 0, 0)
    xhat = (x_in[...].astype(F32) - mu) * inv
    mean_dh = jnp.mean(dh, axis=1, keepdims=True)
    mean_dot = jnp.mean(dh * xhat, axis=1, keepdims=True)
    dx = (g_in[...].astype(F32) + inv * (dh - mean_dh - xhat * mean_dot)).astype(BF16)
    stage(dx, pay_dx, landed_dx)

    for copy in rep_copies:
        copy.wait_recv()
    partial = own[...]
    for t in range(reps - 1):
        partial = partial + rep_in[t].astype(F32)
    own[...] = partial
    kept = pl.ds(pl.multiple_of(core * half, half), half)
    core_out[...] = own[pl.ds(pl.multiple_of((1 - core) * half, half), half), :].astype(BF16)
    to_core = send(core_out, core_in, core_sems.at[0], core_sems.at[1], partner)
    middle = len(mates) // 2
    dx_copies = give_back(pay_dx, landed_dx, dx_sems, range(middle))

    to_core.wait_recv()
    partial = own[kept, :] + core_in[...].astype(F32)
    own[0:half, :] = partial
    z_out[...] = partial.astype(BF16)
    z_copies = []
    for k, other in enumerate(along_z):
        there = pl.ds(pl.multiple_of(other * piece, piece), piece)
        z_copies.append(
            send(z_out.at[there, :], z_in.at[k], z_sems.at[0, k], z_sems.at[1, k], (base + CORES * other + core, rep))
        )
    dx_copies += give_back(pay_dx, landed_dx, dx_sems, range(middle, len(mates)))

    for copy in z_copies:
        copy.wait_recv()
    summed = own[pl.ds(pl.multiple_of(z * piece, piece), piece), :]
    for k in range(depth - 1):
        summed = summed + z_in[k].astype(F32)
    x_all[row] = summed
    row_copies = [
        send(x_all.at[row], x_all.at[row], row_sems.at[0, k], row_sems.at[1, k], peer)
        for k, peer in enumerate(peers_x)
    ]
    for copy in out_copies:
        copy.wait_recv()
    out_ref[...] = unpack_all(landed_out, place, depth).astype(BF16)
    for copy in row_copies:
        copy.wait_recv()
    summed = x_all[0]
    for k in range(1, reps):
        summed = summed + x_all[k]
    done = pl.ds(pl.multiple_of(core * half + z * piece, piece), piece)
    total[done, :] = summed.astype(BF16)
    all_copies = [
        send(
            total.at[done, :], total.at[done, :], all_sems.at[0, k], all_sems.at[1, k],
            (base + CORES * other + core, rep),
        )
        for k, other in enumerate(along_z)
    ]
    span = slots // depth
    lines = group * reps * small // depth
    for dz in reversed(far_first(depth)):
        for copy, (step, _) in zip(dx_copies, ends):
            if step == dz:
                copy.wait_recv()
        source = lax.rem(z + depth - dz, depth)
        landed_rows = landed_dx[pl.ds(pl.multiple_of(source * lines, lines), lines), :]
        part = unpack(landed_rows, place[pl.ds(pl.multiple_of(source * span, span), span), :])
        if dz:
            gin_ref[...] += part
        else:
            gin_ref[...] = part
    for copy in all_copies:
        copy.wait_recv()
    last = send(total.at[kept, :], total.at[kept, :], last_sems.at[0], last_sems.at[1], partner)
    last.wait_recv()
    for i in range(3):
        gqkv_ref[i] = total[width * i : width * (i + 1), :].astype(F32)
    gproj_ref[...] = total[3 * width :, :].astype(F32)
    for copy in (
        w_copies + x_copies + g_copies + out_copies + dx_copies + rep_copies
        + [to_core] + z_copies + row_copies + all_copies + [last]
    ):
        copy.wait_send()


def copy_kernel(*refs):
    count = len(refs) // 2
    sources, targets, sems = refs[:count], refs[count : 2 * count], refs[2 * count]
    copies = [pltpu.make_async_copy(a, b, sems.at[i]) for i, (a, b) in enumerate(zip(sources, targets))]
    for copy in copies:
        copy.start()
    for copy in copies:
        copy.wait()


def copy_out(arrays):
    return pl.pallas_call(
        copy_kernel,
        out_shape=[jax.ShapeDtypeStruct(a.shape, a.dtype) for a in arrays],
        in_specs=[pl.BlockSpec(memory_space=pl.ANY)] * len(arrays),
        out_specs=[pl.BlockSpec(memory_space=pl.ANY)] * len(arrays),
        scratch_shapes=[pltpu.SemaphoreType.DMA((len(arrays),))],
        compiler_params=pltpu.CompilerParams(vmem_limit_bytes=1 << 20),
    )(*arrays)


def shards(reps, group, points, counts, order, grad_out, w_qkv, w_proj):
    slots, channels = points.shape
    patch = slots // reps
    width = channels // reps
    half = 2 * width
    piece = half // (group // CORES)
    heads = channels // HEAD
    dma = pltpu.SemaphoreType.DMA
    vmem = pltpu.VMEM
    anywhere = pl.BlockSpec(memory_space=pl.ANY)
    results = pl.pallas_call(
        functools.partial(block_kernel, reps, group),
        out_shape=[
            jax.ShapeDtypeStruct((width, slots), BF16),
            jax.ShapeDtypeStruct((width, slots), F32),
            jax.ShapeDtypeStruct((3, width, channels), F32),
            jax.ShapeDtypeStruct((width, channels), F32),
        ],
        in_specs=[anywhere, anywhere, anywhere, SMEM, anywhere, anywhere],
        out_specs=[VMEM] * 4,
        scratch_shapes=[
            vmem((slots, channels), BF16),
            vmem((slots, channels), BF16),
            vmem((1, slots), jnp.int32),
            vmem((slots, 8), jnp.int32),
            vmem((patch, channels), BF16),
            vmem((patch, channels), BF16),
            vmem((patch, channels), BF16),
            vmem((patch, channels), BF16),
            vmem((3, channels, channels), BF16),
            vmem((channels, channels), BF16),
            vmem((slots, slots), BF16),
            vmem((3 * channels, patch), BF16),
            vmem((channels, patch), BF16),
            vmem((patch, patch), F32),
            vmem((2, patch, patch), F32),
            vmem((channels, patch), BF16),
            vmem((channels, patch), F32),
            vmem((3 * channels, patch), BF16),
            vmem((patch, channels), BF16),
            vmem((heads, patch, patch), BF16),
            vmem((heads, patch), F32),
            vmem((reps, patch // 2, 2 * width), BF16),
            vmem((reps, patch // 2, 2 * width), BF16),
            vmem((slots // 2, 2 * width), BF16),
            vmem((slots // 2, 2 * width), BF16),
            vmem((reps - 1, 4 * width, channels), BF16),
            vmem((reps - 1, 4 * width, channels), BF16),
            vmem((half, channels), BF16),
            vmem((half, channels), BF16),
            vmem((4 * width, channels), F32),
            vmem((half, channels), BF16),
            vmem((group // CORES - 1, piece, channels), BF16),
            vmem((reps, piece, channels), F32),
            vmem((4 * width, channels), BF16),
            dma((5,)),
            dma((2, reps - 1)),
            dma((2, reps - 1)),
            dma((2, group - 1)),
            dma((2, group - 1)),
            dma((2, group * reps - 1)),
            dma((2, group * reps - 1)),
            dma((2, reps - 1)),
            dma((2,)),
            dma((2, group // CORES - 1)),
            dma((2, reps - 1)),
            dma((2, group // CORES - 1)),
            dma((2,)),
        ],
        compiler_params=pltpu.CompilerParams(
            collective_id=0, has_side_effects=True, vmem_limit_bytes=52 << 20
        ),
    )(points, grad_out, order.reshape(1, slots), counts, w_qkv.transpose(0, 2, 1), w_proj)
    out, grad_input, grad_qkv, grad_proj = copy_out(results)
    return out.T, grad_input.T, grad_qkv.transpose(0, 2, 1), grad_proj


def solution(mesh):
    reps = mesh.shape["rep"]
    group = mesh.shape["pts"] // reps
    return jax.shard_map(
        functools.partial(shards, reps, group),
        mesh=mesh,
        in_specs=(
            P("pts", None),
            P("pts"),
            P("pts"),
            P("pts", None),
            P(None, None, "rep"),
            P("rep", None),
        ),
        out_specs=(P("pts", "rep"), P("pts", "rep"), P(None, None, "rep"), P("rep", None)),
        check_vma=False,
    )
```

```python
import functools

import jax
import jax.numpy as jnp
from jax import lax
from jax.experimental import pallas as pl
from jax.experimental.pallas import tpu as pltpu
from jax.sharding import PartitionSpec as P

HEAD = 16
CORES = 2
SCALE = 0.25
EPS = 1e-05
NEGATIVE = -1e30
DEAD = 64.0
ALIVE_BELOW = 32.0
F32, BF16 = jnp.float32, jnp.bfloat16
MESH = pl.DeviceIdType.MESH
VMEM = pl.BlockSpec(memory_space=pltpu.VMEM)
SMEM = pl.BlockSpec(memory_space=pltpu.SMEM)


def dot(a, b, ca=1, cb=0):
    return lax.dot_general(a, b, (((ca,), (cb,)), ((), ())), preferred_element_type=F32)


def column(row):
    wide = jnp.broadcast_to(row.astype(F32), (8, row.shape[1]))
    return wide.T[:, 0:1].astype(jnp.int32)


def send(src, dst, send_sem, recv_sem, peer):
    copy = pltpu.make_async_remote_copy(
        src_ref=src, dst_ref=dst, send_sem=send_sem, recv_sem=recv_sem,
        device_id=peer, device_id_type=MESH,
    )
    copy.start()
    return copy


def far_first(n):
    return sorted(range(n), key=lambda k: -min(k, n - k))


def pack(array, width, first, group):
    rows = array.shape[0]
    cut = array[:, first : first + width].reshape(group, 2, rows // group // 2, width)
    return jnp.concatenate([cut[:, 0].reshape(rows // 2, width), cut[:, 1].reshape(rows // 2, width)], axis=1)


def unpack(landed, place):
    width = landed.shape[1] // 2
    halves = landed.T
    return dot(jnp.concatenate([halves[:width], halves[width:]], axis=1), place)


def unpack_all(landed, place, depth):
    width = landed.shape[1] // 2
    halves = landed[...].T
    lines = landed.shape[0] // depth
    cuts = [
        halves[width * h : width * (h + 1), lines * zz : lines * (zz + 1)] for zz in range(depth) for h in range(2)
    ]
    return dot(jnp.concatenate(cuts, axis=1), place[...])


def block_kernel(
    reps, group, points_hbm, grads_hbm, order_hbm, counts_ref, w_hbm, wp_hbm,
    out_ref, gin_ref, gqkv_ref, gproj_ref,
    points, grads, order, target, xs, gs, x_in, g_in, w_all, wp_all, place,
    qkv, da, bias, scores, at, a_full, dqkv, hbuf, probs, recips,
    pay_out, pay_dx, landed_out, landed_dx,
    rep_out, rep_in, core_out, core_in, own, z_out, z_in, x_all, total,
    load_sems, w_sems, wp_sems, x_sems, g_sems, out_sems, dx_sems, rep_sems,
    core_sems, z_sems, row_sems, all_sems, last_sems,
):
    me, rep = lax.axis_index("pts"), lax.axis_index("rep")
    member = lax.rem(me, group)
    base = me - member
    row = me // group
    slots, channels = points.shape
    patch = x_in.shape[0]
    block = patch // group
    width = channels // reps
    half = 2 * width
    depth = group // CORES
    piece = half // depth
    z, core = member // CORES, lax.rem(member, CORES)
    partner = (base + CORES * z + 1 - core, rep)

    def moved(dz, dc):
        return CORES * lax.rem(z + dz, depth) + lax.rem(core + dc, CORES)

    steps = [(dz, dc) for dz in far_first(depth) for dc in range(CORES)]
    along = [moved(dz, dc) for dz, dc in steps if dz or dc]
    along_z = [lax.rem(z + dz, depth) for dz in far_first(depth) if dz]
    beside = [(me, lax.rem(rep + k, reps)) for k in far_first(reps) if k]
    mates = [
        (lax.rem(rep + k, reps), moved(dz, dc))
        for dz, dc in steps for k in far_first(reps) if k or dz or dc
    ]
    ends = [step for step in steps for k in far_first(reps) if k or step != (0, 0)]
    peers_x = [(lax.rem(row + k, reps) * group + member, rep) for k in far_first(reps) if k]

    mine = pl.ds(pl.multiple_of(rep * width, width), width)
    loads = []
    for i, (source, target_ref) in enumerate((
        (order_hbm, order), (points_hbm, points), (grads_hbm, grads),
        (w_hbm, w_all.at[:, mine, :]), (wp_hbm, wp_all.at[mine, :]),
    )):
        loads.append(pltpu.make_async_copy(source, target_ref, load_sems.at[i]))
        loads[-1].start()
    barrier = pltpu.get_barrier_semaphore()
    peers = [(base + n, rep) for n in along] + beside + peers_x
    for peer in peers:
        pl.semaphore_signal(barrier, inc=1, device_id=peer, device_id_type=MESH)

    loads[0].wait()
    rows = column(order[:, pl.ds(pl.multiple_of(rep * patch, patch), patch)])
    live = rows < counts_ref[0]
    slot = lax.broadcasted_iota(jnp.int32, (patch, slots), 1)
    pick = jnp.where(rows == slot, 1.0, 0.0).astype(BF16)
    loads[1].wait()
    xs[...] = jnp.where(live, dot(pick, points[...]), DEAD).astype(BF16)
    pl.semaphore_wait(barrier, len(peers))

    sent, w_copies, x_copies, g_copies = [], [], [], []
    for k, peer in enumerate(beside):
        w_copies.append(send(w_hbm, w_all.at[:, mine, :], w_sems.at[0, k], w_sems.at[1, k], peer))
        w_copies.append(send(wp_hbm, wp_all.at[mine, :], wp_sems.at[0, k], wp_sems.at[1, k], peer))
    here = pl.ds(pl.multiple_of(member * block, block), block)

    def scatter(staged, landed, sems, copies):
        for k, other in enumerate(along):
            there = pl.ds(pl.multiple_of(other * block, block), block)
            copies.append(
                send(staged.at[there, :], landed.at[here, :], sems.at[0, k], sems.at[1, k], (base + other, rep))
            )
        landed[here, :] = staged[here, :]

    scatter(xs, x_in, x_sems, x_copies)
    loads[2].wait()
    gs[...] = jnp.where(live, dot(pick, grads[...]), 0.0).astype(BF16)

    whole = column(order[...])
    small = block // 2
    first = 0
    for zz in range(depth):
        for hh in range(2):
            for cc in range(CORES):
                for k in range(reps):
                    start = ((k * depth + zz) * CORES + cc) * block + hh * small
                    target[first : first + small, :] = jnp.broadcast_to(whole[start : start + small], (small, 8))
                    first += small
    chunk = 128

    def fill(c, _):
        rows = pl.ds(pl.multiple_of(c * chunk, chunk), chunk)
        arrival = lax.broadcasted_iota(jnp.int32, (chunk, slots), 1)
        place[rows, :] = jnp.where(target[rows, 0:1] == arrival, 1.0, 0.0).astype(BF16)
        return 0

    lax.fori_loop(0, slots // chunk, fill, 0)

    for copy in x_copies:
        copy.wait_recv()
    scatter(gs, g_in, g_sems, g_copies)
    x = x_in[...].astype(F32)
    mu = jnp.mean(x, axis=1, keepdims=True)
    centered = x - mu
    inv = lax.rsqrt(jnp.mean(centered * centered, axis=1, keepdims=True) + EPS)
    hbuf[...] = (centered * inv).astype(BF16)
    keep = x[:, 0:1] < ALIVE_BELOW
    key = lax.broadcasted_iota(jnp.int32, (patch, patch), 0)
    query = lax.broadcasted_iota(jnp.int32, (patch, patch), 1)
    bias[...] = jnp.where(keep | (key == query), 0.0, NEGATIVE)
    loads[3].wait()
    loads[4].wait()
    for copy in w_copies:
        copy.wait_recv()
    projected = dot(w_all[...].reshape(3 * channels, channels), hbuf[...], 1, 1).astype(BF16)
    qkv[0:channels, :] = (projected[0:channels] * SCALE).astype(BF16)
    qkv[channels:, :] = projected[channels:]
    ones = jnp.ones((HEAD, patch), BF16)

    def heads(n):
        o = pl.multiple_of(n * HEAD, HEAD)
        return (
            pl.ds(o, HEAD), qkv[pl.ds(o, HEAD), :],
            qkv[pl.ds(channels + o, HEAD), :], qkv[pl.ds(2 * channels + o, HEAD), :],
        )

    def score(n):
        _, qh, kh, _ = heads(n)
        return dot(kh, qh, 0, 0) + bias[...]

    def mix(n, s):
        rows, _, _, vh = heads(n)
        e = jnp.exp(s - jnp.max(s, axis=0, keepdims=True)).astype(BF16)
        probs[n] = e
        mixed = dot(jnp.concatenate([vh, ones], axis=0), e)
        recip = 1.0 / mixed[HEAD : HEAD + 1]
        a = mixed[0:HEAD] * recip
        recips[pl.ds(n, 1), :] = recip
        a_full[rows, :] = a
        at[rows, :] = a.astype(BF16)

    count = channels // HEAD
    unrolled = 8

    def forward(i, _):
        for j in range(unrolled):
            n = i * unrolled + j
            follower = lax.rem(n + 1, count) if j == unrolled - 1 else n + 1
            scores[(j + 1) % 2] = score(follower)
            mix(n, scores[j % 2])
        return 0

    scores[0] = score(0)
    lax.fori_loop(0, count // unrolled, forward, 0)
    x = x_in[...].astype(F32)
    out = (keep.astype(F32) * (x + dot(at[...], wp_all[...], 0, 0))).astype(BF16)
    back = pl.ds(pl.multiple_of((member * reps + rep) * small, small), small)

    def stage(array, pay, landed):
        for r in range(reps):
            pay[r] = pack(array, width, width * r, group)
        landed[back, :] = pay[rep, pl.ds(pl.multiple_of(member * small, small), small), :]

    def give_back(pay, landed, sems, which):
        copies = []
        for i in which:
            k, n = mates[i]
            there = pl.ds(pl.multiple_of(n * small, small), small)
            copies.append(
                send(pay.at[k, there, :], landed.at[back, :], sems.at[0, i], sems.at[1, i], (base + n, k))
            )
        return copies

    stage(out, pay_out, landed_out)
    out_copies = give_back(pay_out, landed_out, out_sems, range(len(mates)))

    for copy in g_copies:
        copy.wait_recv()
    da[...] = dot(wp_all[...], g_in[...], 1, 1).astype(BF16)

    def backward(n):
        rows, qh, kh, vh = heads(n)
        dahf = da[rows, :].astype(F32) * recips[pl.ds(n, 1), :]
        dah = dahf.astype(BF16)
        delta = jnp.sum(dahf * a_full[rows, :], axis=0, keepdims=True)
        e = probs[n]
        o = pl.multiple_of(n * HEAD, HEAD)
        dp = dot(vh, dah, 0, 0)
        dqkv[pl.ds(2 * channels + o, HEAD), :] = dot(dah, e, 1, 1).astype(BF16)
        ds = (e.astype(F32) * (dp - delta)).astype(BF16)
        dqkv[pl.ds(o, HEAD), :] = (dot(kh, ds) * SCALE).astype(BF16)
        dqkv[pl.ds(channels + o, HEAD), :] = dot(qh, ds, 1, 1).astype(BF16)

    rep_copies = []
    parts = 2
    per = width // HEAD // parts
    thin = per * HEAD
    for t in range(reps):
        part = lax.rem(rep + 1 + t, reps)
        for u in range(parts):
            for i in range(per):
                backward((part * parts + u) * per + i)
            first = pl.multiple_of((part * parts + u) * thin, thin)
            grown = [dqkv[pl.ds(channels * i + first, thin), :] for i in range(3)]
            grad_w = dot(jnp.concatenate(grown, axis=0), hbuf[...])
            grad_p = dot(at[pl.ds(first, thin), :], g_in[...])
            lines = slice(4 * thin * u, 4 * thin * (u + 1))
            if t < reps - 1:
                i = t * parts + u
                rep_out[t, lines, :] = jnp.concatenate([grad_w, grad_p], axis=0).astype(BF16)
                rep_copies.append(
                    send(rep_out.at[t, lines, :], rep_in.at[t, lines, :], rep_sems.at[0, i], rep_sems.at[1, i], (me, part))
                )
            else:
                own[lines, :] = jnp.concatenate([grad_w, grad_p], axis=0)

    dh = dot(dqkv[...], w_all[...].reshape(3 * channels, channels), 0, 0)
    xhat = (x_in[...].astype(F32) - mu) * inv
    mean_dh = jnp.mean(dh, axis=1, keepdims=True)
    mean_dot = jnp.mean(dh * xhat, axis=1, keepdims=True)
    dx = (g_in[...].astype(F32) + inv * (dh - mean_dh - xhat * mean_dot)).astype(BF16)
    stage(dx, pay_dx, landed_dx)

    for copy in rep_copies:
        copy.wait_recv()
    partial = own[...]
    for t in range(reps - 1):
        partial = partial + rep_in[t].astype(F32)
    own[...] = partial
    kept = pl.ds(pl.multiple_of(core * half, half), half)
    core_out[...] = own[pl.ds(pl.multiple_of((1 - core) * half, half), half), :].astype(BF16)
    to_core = send(core_out, core_in, core_sems.at[0], core_sems.at[1], partner)
    to_core.wait_recv()
    partial = own[kept, :] + core_in[...].astype(F32)
    own[0:half, :] = partial
    z_out[...] = partial.astype(BF16)
    z_copies = []
    for k, other in enumerate(along_z):
        there = pl.ds(pl.multiple_of(other * piece, piece), piece)
        z_copies.append(
            send(z_out.at[there, :], z_in.at[k], z_sems.at[0, k], z_sems.at[1, k], (base + CORES * other + core, rep))
        )
    dx_copies = give_back(pay_dx, landed_dx, dx_sems, range(len(mates)))

    for copy in z_copies:
        copy.wait_recv()
    summed = own[pl.ds(pl.multiple_of(z * piece, piece), piece), :]
    for k in range(depth - 1):
        summed = summed + z_in[k].astype(F32)
    x_all[row] = summed
    row_copies = [
        send(x_all.at[row], x_all.at[row], row_sems.at[0, k], row_sems.at[1, k], peer)
        for k, peer in enumerate(peers_x)
    ]
    for copy in out_copies:
        copy.wait_recv()
    out_ref[...] = unpack_all(landed_out, place, depth).astype(BF16)
    for copy in row_copies:
        copy.wait_recv()
    summed = x_all[0]
    for k in range(1, reps):
        summed = summed + x_all[k]
    done = pl.ds(pl.multiple_of(core * half + z * piece, piece), piece)
    total[done, :] = summed.astype(BF16)
    all_copies = [
        send(
            total.at[done, :], total.at[done, :], all_sems.at[0, k], all_sems.at[1, k],
            (base + CORES * other + core, rep),
        )
        for k, other in enumerate(along_z)
    ]
    span = slots // depth
    lines = group * reps * small // depth
    for dz in reversed(far_first(depth)):
        for copy, (step, _) in zip(dx_copies, ends):
            if step == dz:
                copy.wait_recv()
        source = lax.rem(z + depth - dz, depth)
        landed_rows = landed_dx[pl.ds(pl.multiple_of(source * lines, lines), lines), :]
        part = unpack(landed_rows, place[pl.ds(pl.multiple_of(source * span, span), span), :])
        if dz:
            gin_ref[...] += part
        else:
            gin_ref[...] = part
    for copy in all_copies:
        copy.wait_recv()
    last = send(total.at[kept, :], total.at[kept, :], last_sems.at[0], last_sems.at[1], partner)
    last.wait_recv()
    for u in range(parts):
        for i in range(4):
            first = (u * 4 + i) * thin
            grown = total[first : first + thin, :].astype(F32)
            if i < 3:
                gqkv_ref[i, thin * u : thin * (u + 1), :] = grown
            else:
                gproj_ref[thin * u : thin * (u + 1), :] = grown
    for copy in (
        w_copies + x_copies + g_copies + out_copies + dx_copies + rep_copies
        + [to_core] + z_copies + row_copies + all_copies + [last]
    ):
        copy.wait_send()


def copy_kernel(*refs):
    count = len(refs) // 2
    sources, targets, sems = refs[:count], refs[count : 2 * count], refs[2 * count]
    copies = [pltpu.make_async_copy(a, b, sems.at[i]) for i, (a, b) in enumerate(zip(sources, targets))]
    for copy in copies:
        copy.start()
    for copy in copies:
        copy.wait()


def copy_out(arrays):
    return pl.pallas_call(
        copy_kernel,
        out_shape=[jax.ShapeDtypeStruct(a.shape, a.dtype) for a in arrays],
        in_specs=[pl.BlockSpec(memory_space=pl.ANY)] * len(arrays),
        out_specs=[pl.BlockSpec(memory_space=pl.ANY)] * len(arrays),
        scratch_shapes=[pltpu.SemaphoreType.DMA((len(arrays),))],
        compiler_params=pltpu.CompilerParams(vmem_limit_bytes=1 << 20),
    )(*arrays)


def shards(reps, group, points, counts, order, grad_out, w_qkv, w_proj):
    slots, channels = points.shape
    patch = slots // reps
    width = channels // reps
    half = 2 * width
    piece = half // (group // CORES)
    heads = channels // HEAD
    dma = pltpu.SemaphoreType.DMA
    vmem = pltpu.VMEM
    anywhere = pl.BlockSpec(memory_space=pl.ANY)
    results = pl.pallas_call(
        functools.partial(block_kernel, reps, group),
        out_shape=[
            jax.ShapeDtypeStruct((width, slots), BF16),
            jax.ShapeDtypeStruct((width, slots), F32),
            jax.ShapeDtypeStruct((3, width, channels), F32),
            jax.ShapeDtypeStruct((width, channels), F32),
        ],
        in_specs=[anywhere, anywhere, anywhere, SMEM, anywhere, anywhere],
        out_specs=[VMEM] * 4,
        scratch_shapes=[
            vmem((slots, channels), BF16),
            vmem((slots, channels), BF16),
            vmem((1, slots), jnp.int32),
            vmem((slots, 8), jnp.int32),
            vmem((patch, channels), BF16),
            vmem((patch, channels), BF16),
            vmem((patch, channels), BF16),
            vmem((patch, channels), BF16),
            vmem((3, channels, channels), BF16),
            vmem((channels, channels), BF16),
            vmem((slots, slots), BF16),
            vmem((3 * channels, patch), BF16),
            vmem((channels, patch), BF16),
            vmem((patch, patch), F32),
            vmem((2, patch, patch), F32),
            vmem((channels, patch), BF16),
            vmem((channels, patch), F32),
            vmem((3 * channels, patch), BF16),
            vmem((patch, channels), BF16),
            vmem((heads, patch, patch), BF16),
            vmem((heads, patch), F32),
            vmem((reps, patch // 2, 2 * width), BF16),
            vmem((reps, patch // 2, 2 * width), BF16),
            vmem((slots // 2, 2 * width), BF16),
            vmem((slots // 2, 2 * width), BF16),
            vmem((reps - 1, 4 * width, channels), BF16),
            vmem((reps - 1, 4 * width, channels), BF16),
            vmem((half, channels), BF16),
            vmem((half, channels), BF16),
            vmem((4 * width, channels), F32),
            vmem((half, channels), BF16),
            vmem((group // CORES - 1, piece, channels), BF16),
            vmem((reps, piece, channels), F32),
            vmem((4 * width, channels), BF16),
            dma((5,)),
            dma((2, reps - 1)),
            dma((2, reps - 1)),
            dma((2, group - 1)),
            dma((2, group - 1)),
            dma((2, group * reps - 1)),
            dma((2, group * reps - 1)),
            dma((2, 2 * (reps - 1))),
            dma((2,)),
            dma((2, group // CORES - 1)),
            dma((2, reps - 1)),
            dma((2, group // CORES - 1)),
            dma((2,)),
        ],
        compiler_params=pltpu.CompilerParams(
            collective_id=0, has_side_effects=True, vmem_limit_bytes=52 << 20
        ),
    )(points, grad_out, order.reshape(1, slots), counts, w_qkv.transpose(0, 2, 1), w_proj)
    out, grad_input, grad_qkv, grad_proj = copy_out(results)
    return out.T, grad_input.T, grad_qkv.transpose(0, 2, 1), grad_proj


def solution(mesh):
    reps = mesh.shape["rep"]
    group = mesh.shape["pts"] // reps
    return jax.shard_map(
        functools.partial(shards, reps, group),
        mesh=mesh,
        in_specs=(
            P("pts", None),
            P("pts"),
            P("pts"),
            P("pts", None),
            P(None, None, "rep"),
            P("rep", None),
        ),
        out_specs=(P("pts", "rep"), P("pts", "rep"), P(None, None, "rep"), P("rep", None)),
        check_vma=False,
    )
```

```python
import functools

import jax
import jax.numpy as jnp
from jax import lax
from jax.experimental import pallas as pl
from jax.experimental.pallas import tpu as pltpu
from jax.sharding import PartitionSpec as P

HEAD = 16
CORES = 2
SCALE = 0.25
EPS = 1e-05
NEGATIVE = -1e30
DEAD = 64.0
ALIVE_BELOW = 32.0
DIGIT = 64
LANES = 128
F32, BF16 = jnp.float32, jnp.bfloat16
MESH = pl.DeviceIdType.MESH
VMEM = pl.BlockSpec(memory_space=pltpu.VMEM)
SMEM = pl.BlockSpec(memory_space=pltpu.SMEM)


def dot(a, b, ca=1, cb=0):
    return lax.dot_general(a, b, (((ca,), (cb,)), ((), ())), preferred_element_type=F32)


def send(src, dst, send_sem, recv_sem, peer):
    copy = pltpu.make_async_remote_copy(
        src_ref=src, dst_ref=dst, send_sem=send_sem, recv_sem=recv_sem,
        device_id=peer, device_id_type=MESH,
    )
    copy.start()
    return copy


def far_first(n):
    return sorted(range(n), key=lambda k: -min(k, n - k))


def pack(array, width, first, group):
    rows = array.shape[0]
    cut = array[:, first : first + width].reshape(group, 2, rows // group // 2, width)
    return jnp.concatenate([cut[:, 0].reshape(rows // 2, width), cut[:, 1].reshape(rows // 2, width)], axis=1)


def unpack(landed, place):
    width = landed.shape[1] // 2
    halves = landed.T
    return dot(jnp.concatenate([halves[:width], halves[width:]], axis=1), place)


def unpack_all(landed, place, depth):
    width = landed.shape[1] // 2
    halves = landed[...].T
    lines = landed.shape[0] // depth
    cuts = [
        halves[width * h : width * (h + 1), lines * zz : lines * (zz + 1)] for zz in range(depth) for h in range(2)
    ]
    return dot(jnp.concatenate(cuts, axis=1), place[...])


def block_kernel(
    reps, group, points_hbm, grads_hbm, counts_ref, mixed_hbm,
    out_ref, gin_ref, gqkv_ref, gproj_ref,
    points, grads, digits, order, target, xs, gs, x_in, g_in, w_all, place,
    qkv, da, bias, scores, at, a_full, dqkv, hbuf, probs, recips,
    pay_out, pay_dx, landed_out, landed_dx,
    core_out, core_in, own, z_out, z_in, row_out, row_all, total,
    load_sems, w_sems, x_sems, g_sems, out_sems, dx_sems,
    core_sems, z_sems, row_sems, all_sems, last_sems,
):
    me, rep = lax.axis_index("pts"), lax.axis_index("rep")
    member = lax.rem(me, group)
    base = me - member
    row = me // group
    slots, channels = points.shape
    patch = x_in.shape[0]
    block = patch // group
    width = channels // reps
    half = 2 * width
    depth = group // CORES
    piece = half // depth
    z, core = member // CORES, lax.rem(member, CORES)
    partner = (base + CORES * z + 1 - core, rep)

    def moved(dz, dc):
        return CORES * lax.rem(z + dz, depth) + lax.rem(core + dc, CORES)

    steps = [(dz, dc) for dz in far_first(depth) for dc in range(CORES)]
    along = [moved(dz, dc) for dz, dc in steps if dz or dc]
    along_z = [lax.rem(z + dz, depth) for dz in far_first(depth) if dz]
    beside = [(me, lax.rem(rep + k, reps)) for k in far_first(reps) if k]
    mates = [
        (lax.rem(rep + k, reps), moved(dz, dc))
        for dz, dc in steps for k in far_first(reps) if k or dz or dc
    ]
    ends = [step for step in steps for k in far_first(reps) if k or step != (0, 0)]
    peers_x = [(lax.rem(row + k, reps) * group + member, rep) for k in far_first(reps) if k]

    w_mine = mixed_hbm.at[0 : 4 * width, :]
    loads = []
    for i, (source, target_ref) in enumerate((
        (mixed_hbm.at[4 * width :, :], digits), (points_hbm, points), (grads_hbm, grads),
        (w_mine, w_all.at[rep]),
    )):
        loads.append(pltpu.make_async_copy(source, target_ref, load_sems.at[i]))
        loads[-1].start()
    barrier = pltpu.get_barrier_semaphore()
    peers = [(base + n, rep) for n in along] + beside + peers_x
    for peer in peers:
        pl.semaphore_signal(barrier, inc=1, device_id=peer, device_id_type=MESH)

    loads[0].wait()
    both = digits[...].astype(F32)
    turned = (both[:, :LANES] * DIGIT + both[:, LANES:]).T
    for j in range(slots // LANES):
        order[LANES * j : LANES * (j + 1), :] = jnp.broadcast_to(turned[:, j : j + 1], (LANES, 8)).astype(jnp.int32)
    rows = order[pl.ds(pl.multiple_of(rep * patch, patch), patch), 0:1]
    live = rows < counts_ref[0]
    slot = lax.broadcasted_iota(jnp.int32, (patch, slots), 1)
    pick = jnp.where(rows == slot, 1.0, 0.0).astype(BF16)
    loads[1].wait()
    xs[...] = jnp.where(live, dot(pick, points[...]), DEAD).astype(BF16)
    pl.semaphore_wait(barrier, len(peers))

    sent, w_copies, x_copies, g_copies = [], [], [], []
    for k, peer in enumerate(beside):
        w_copies.append(send(w_mine, w_all.at[rep], w_sems.at[0, k], w_sems.at[1, k], peer))
    here = pl.ds(pl.multiple_of(member * block, block), block)

    def scatter(staged, landed, sems, copies):
        for k, other in enumerate(along):
            there = pl.ds(pl.multiple_of(other * block, block), block)
            copies.append(
                send(staged.at[there, :], landed.at[here, :], sems.at[0, k], sems.at[1, k], (base + other, rep))
            )
        landed[here, :] = staged[here, :]

    scatter(xs, x_in, x_sems, x_copies)
    loads[2].wait()
    gs[...] = jnp.where(live, dot(pick, grads[...]), 0.0).astype(BF16)

    small = block // 2
    first = 0
    for zz in range(depth):
        for hh in range(2):
            for cc in range(CORES):
                for k in range(reps):
                    start = ((k * depth + zz) * CORES + cc) * block + hh * small
                    target[first : first + small, :] = order[start : start + small, :]
                    first += small
    chunk = 128

    def fill(c, _):
        rows = pl.ds(pl.multiple_of(c * chunk, chunk), chunk)
        arrival = lax.broadcasted_iota(jnp.int32, (chunk, slots), 1)
        place[rows, :] = jnp.where(target[rows, 0:1] == arrival, 1.0, 0.0).astype(BF16)
        return 0

    lax.fori_loop(0, slots // chunk, fill, 0)

    for copy in x_copies:
        copy.wait_recv()
    scatter(gs, g_in, g_sems, g_copies)
    x = x_in[...].astype(F32)
    mu = jnp.mean(x, axis=1, keepdims=True)
    centered = x - mu
    inv = lax.rsqrt(jnp.mean(centered * centered, axis=1, keepdims=True) + EPS)
    hbuf[...] = (centered * inv).astype(BF16)
    keep = x[:, 0:1] < ALIVE_BELOW
    key = lax.broadcasted_iota(jnp.int32, (patch, patch), 0)
    query = lax.broadcasted_iota(jnp.int32, (patch, patch), 1)
    bias[...] = jnp.where(keep | (key == query), 0.0, NEGATIVE)
    loads[3].wait()
    for copy in w_copies:
        copy.wait_recv()
    def weights(first, last):
        return jnp.concatenate(
            [w_all[k, width * i : width * (i + 1), :] for i in range(first, last) for k in range(reps)], axis=0
        )

    projected = dot(weights(0, 3), hbuf[...], 1, 1).astype(BF16)
    qkv[0:channels, :] = (projected[0:channels] * SCALE).astype(BF16)
    qkv[channels:, :] = projected[channels:]
    ones = jnp.ones((HEAD, patch), BF16)

    def heads(n):
        o = pl.multiple_of(n * HEAD, HEAD)
        return (
            pl.ds(o, HEAD), qkv[pl.ds(o, HEAD), :],
            qkv[pl.ds(channels + o, HEAD), :], qkv[pl.ds(2 * channels + o, HEAD), :],
        )

    def score(n):
        _, qh, kh, _ = heads(n)
        return dot(kh, qh, 0, 0) + bias[...]

    def mix(n, s):
        rows, _, _, vh = heads(n)
        e = jnp.exp(s - jnp.max(s, axis=0, keepdims=True)).astype(BF16)
        probs[n] = e
        mixed = dot(jnp.concatenate([vh, ones], axis=0), e)
        recip = 1.0 / mixed[HEAD : HEAD + 1]
        a = mixed[0:HEAD] * recip
        recips[pl.ds(n, 1), :] = recip
        a_full[rows, :] = a
        at[rows, :] = a.astype(BF16)

    count = channels // HEAD
    unrolled = 8

    def forward(i, _):
        for j in range(unrolled):
            n = i * unrolled + j
            follower = lax.rem(n + 1, count) if j == unrolled - 1 else n + 1
            scores[(j + 1) % 2] = score(follower)
            mix(n, scores[j % 2])
        return 0

    scores[0] = score(0)
    lax.fori_loop(0, count // unrolled, forward, 0)
    x = x_in[...].astype(F32)
    out = (keep.astype(F32) * (x + dot(at[...], weights(3, 4), 0, 0))).astype(BF16)
    back = pl.ds(pl.multiple_of((member * reps + rep) * small, small), small)

    def stage(array, pay, landed):
        for r in range(reps):
            pay[r] = pack(array, width, width * r, group)
        landed[back, :] = pay[rep, pl.ds(pl.multiple_of(member * small, small), small), :]

    def give_back(pay, landed, sems, which):
        copies = []
        for i in which:
            k, n = mates[i]
            there = pl.ds(pl.multiple_of(n * small, small), small)
            copies.append(
                send(pay.at[k, there, :], landed.at[back, :], sems.at[0, i], sems.at[1, i], (base + n, k))
            )
        return copies

    stage(out, pay_out, landed_out)
    out_copies = give_back(pay_out, landed_out, out_sems, range(len(mates)))

    for copy in g_copies:
        copy.wait_recv()
    da[...] = dot(weights(3, 4), g_in[...], 1, 1).astype(BF16)

    def backward(n):
        rows, qh, kh, vh = heads(n)
        dahf = da[rows, :].astype(F32) * recips[pl.ds(n, 1), :]
        dah = dahf.astype(BF16)
        delta = jnp.sum(dahf * a_full[rows, :], axis=0, keepdims=True)
        e = probs[n]
        o = pl.multiple_of(n * HEAD, HEAD)
        dp = dot(vh, dah, 0, 0)
        dqkv[pl.ds(2 * channels + o, HEAD), :] = dot(dah, e, 1, 1).astype(BF16)
        ds = (e.astype(F32) * (dp - delta)).astype(BF16)
        dqkv[pl.ds(o, HEAD), :] = (dot(kh, ds) * SCALE).astype(BF16)
        dqkv[pl.ds(channels + o, HEAD), :] = dot(qh, ds, 1, 1).astype(BF16)

    core_copies, z_copies, row_copies = [], [], []
    kept = pl.ds(pl.multiple_of(core * half, half), half)

    def to_core(t):
        core_out[t] = own[t, pl.ds(pl.multiple_of((1 - core) * half, half), half), :].astype(BF16)
        core_copies.append(send(core_out.at[t], core_in.at[t], core_sems.at[0, t], core_sems.at[1, t], partner))

    def to_z(t):
        core_copies[t].wait_recv()
        partial = own[t, kept, :] + core_in[t].astype(F32)
        own[t, 0:half, :] = partial
        z_out[t] = partial.astype(BF16)
        for k, other in enumerate(along_z):
            there = pl.ds(pl.multiple_of(other * piece, piece), piece)
            i = t * (depth - 1) + k
            z_copies.append(
                send(
                    z_out.at[t, there, :], z_in.at[t, k], z_sems.at[0, i], z_sems.at[1, i],
                    (base + CORES * other + core, rep),
                )
            )

    def to_rows(t):
        summed = own[t, pl.ds(pl.multiple_of(z * piece, piece), piece), :]
        for k in range(depth - 1):
            z_copies[t * (depth - 1) + k].wait_recv()
            summed = summed + z_in[t, k].astype(F32)
        row_out[t] = summed
        if t == reps - 1:
            row_all[row, rep] = summed
        for k in far_first(reps):
            if k or t < reps - 1:
                i = t * reps + k
                row_copies.append(
                    send(
                        row_out.at[t], row_all.at[row, rep], row_sems.at[0, i], row_sems.at[1, i],
                        (lax.rem(row + k, reps) * group + member, lax.rem(rep + 1 + t, reps)),
                    )
                )

    per = width // HEAD
    for t in range(reps):
        part = lax.rem(rep + 1 + t, reps)
        for i in range(per):
            backward(part * per + i)
            if t and i == per // 2 - 1:
                to_z(t - 1)
        first = pl.multiple_of(part * width, width)
        grown = [dqkv[pl.ds(channels * i + first, width), :] for i in range(3)]
        own[t, 0 : 3 * width, :] = dot(jnp.concatenate(grown, axis=0), hbuf[...])
        own[t, 3 * width :, :] = dot(at[pl.ds(first, width), :], g_in[...])
        to_core(t)
        if t > 1:
            to_rows(t - 2)

    dh = dot(dqkv[...], weights(0, 3), 0, 0)
    xhat = (x_in[...].astype(F32) - mu) * inv
    mean_dh = jnp.mean(dh, axis=1, keepdims=True)
    mean_dot = jnp.mean(dh * xhat, axis=1, keepdims=True)
    to_z(reps - 1)
    dx = (g_in[...].astype(F32) + inv * (dh - mean_dh - xhat * mean_dot)).astype(BF16)
    stage(dx, pay_dx, landed_dx)
    dx_copies = give_back(pay_dx, landed_dx, dx_sems, range(len(mates)))
    to_rows(reps - 2)
    to_rows(reps - 1)
    for copy in out_copies:
        copy.wait_recv()
    out_ref[...] = unpack_all(landed_out, place, depth).astype(BF16)
    for copy in row_copies:
        copy.wait_recv()
    summed = row_all[0, 0]
    for k in range(1, reps * reps):
        summed = summed + row_all[k // reps, k % reps]
    done = pl.ds(pl.multiple_of(core * half + z * piece, piece), piece)
    total[done, :] = summed.astype(BF16)
    all_copies = [
        send(
            total.at[done, :], total.at[done, :], all_sems.at[0, k], all_sems.at[1, k],
            (base + CORES * other + core, rep),
        )
        for k, other in enumerate(along_z)
    ]
    span = slots // depth
    lines = group * reps * small // depth
    for dz in reversed(far_first(depth)):
        for copy, (step, _) in zip(dx_copies, ends):
            if step == dz:
                copy.wait_recv()
        source = lax.rem(z + depth - dz, depth)
        landed_rows = landed_dx[pl.ds(pl.multiple_of(source * lines, lines), lines), :]
        part = unpack(landed_rows, place[pl.ds(pl.multiple_of(source * span, span), span), :])
        if dz:
            gin_ref[...] += part
        else:
            gin_ref[...] = part
    for copy in all_copies:
        copy.wait_recv()
    last = send(total.at[kept, :], total.at[kept, :], last_sems.at[0], last_sems.at[1], partner)
    last.wait_recv()
    for i in range(3):
        gqkv_ref[i] = total[width * i : width * (i + 1), :].astype(F32)
    gproj_ref[...] = total[3 * width :, :].astype(F32)
    for copy in (
        w_copies + x_copies + g_copies + out_copies + dx_copies
        + core_copies + z_copies + row_copies + all_copies + [last]
    ):
        copy.wait_send()


def copy_kernel(*refs):
    count = len(refs) // 2
    sources, targets, sems = refs[:count], refs[count : 2 * count], refs[2 * count]
    copies = [pltpu.make_async_copy(a, b, sems.at[i]) for i, (a, b) in enumerate(zip(sources, targets))]
    for copy in copies:
        copy.start()
    for copy in copies:
        copy.wait()


def copy_out(arrays):
    return pl.pallas_call(
        copy_kernel,
        out_shape=[jax.ShapeDtypeStruct(a.shape, a.dtype) for a in arrays],
        in_specs=[pl.BlockSpec(memory_space=pl.ANY)] * len(arrays),
        out_specs=[pl.BlockSpec(memory_space=pl.ANY)] * len(arrays),
        scratch_shapes=[pltpu.SemaphoreType.DMA((len(arrays),))],
        compiler_params=pltpu.CompilerParams(vmem_limit_bytes=1 << 20),
    )(*arrays)


def shards(reps, group, points, counts, order, grad_out, w_qkv, w_proj):
    slots, channels = points.shape
    patch = slots // reps
    width = channels // reps
    half = 2 * width
    piece = half // (group // CORES)
    heads = channels // HEAD
    dma = pltpu.SemaphoreType.DMA
    vmem = pltpu.VMEM
    anywhere = pl.BlockSpec(memory_space=pl.ANY)
    order = order.reshape(-1, LANES)
    digits = jnp.concatenate([order // DIGIT, order % DIGIT], axis=1).astype(BF16)
    digits = jnp.pad(digits, ((0, 16 - digits.shape[0]), (0, 0)))
    mixed = jnp.concatenate([w_qkv.transpose(0, 2, 1).reshape(3 * width, channels), w_proj, digits], axis=0)
    results = pl.pallas_call(
        functools.partial(block_kernel, reps, group),
        out_shape=[
            jax.ShapeDtypeStruct((width, slots), BF16),
            jax.ShapeDtypeStruct((width, slots), F32),
            jax.ShapeDtypeStruct((3, width, channels), F32),
            jax.ShapeDtypeStruct((width, channels), F32),
        ],
        in_specs=[anywhere, anywhere, SMEM, anywhere],
        out_specs=[VMEM] * 4,
        scratch_shapes=[
            vmem((slots, channels), BF16),
            vmem((slots, channels), BF16),
            vmem((16, 2 * LANES), BF16),
            vmem((slots, 8), jnp.int32),
            vmem((slots, 8), jnp.int32),
            vmem((patch, channels), BF16),
            vmem((patch, channels), BF16),
            vmem((patch, channels), BF16),
            vmem((patch, channels), BF16),
            vmem((reps, 4 * width, channels), BF16),
            vmem((slots, slots), BF16),
            vmem((3 * channels, patch), BF16),
            vmem((channels, patch), BF16),
            vmem((patch, patch), F32),
            vmem((2, patch, patch), F32),
            vmem((channels, patch), BF16),
            vmem((channels, patch), F32),
            vmem((3 * channels, patch), BF16),
            vmem((patch, channels), BF16),
            vmem((heads, patch, patch), BF16),
            vmem((heads, patch), F32),
            vmem((reps, patch // 2, 2 * width), BF16),
            vmem((reps, patch // 2, 2 * width), BF16),
            vmem((slots // 2, 2 * width), BF16),
            vmem((slots // 2, 2 * width), BF16),
            vmem((reps, half, channels), BF16),
            vmem((reps, half, channels), BF16),
            vmem((reps, 4 * width, channels), F32),
            vmem((reps, half, channels), BF16),
            vmem((reps, group // CORES - 1, piece, channels), BF16),
            vmem((reps, piece, channels), F32),
            vmem((reps, reps, piece, channels), F32),
            vmem((4 * width, channels), BF16),
            dma((4,)),
            dma((2, reps - 1)),
            dma((2, group - 1)),
            dma((2, group - 1)),
            dma((2, group * reps - 1)),
            dma((2, group * reps - 1)),
            dma((2, reps)),
            dma((2, reps * (group // CORES - 1))),
            dma((2, reps * reps)),
            dma((2, group // CORES - 1)),
            dma((2,)),
        ],
        compiler_params=pltpu.CompilerParams(
            collective_id=0, has_side_effects=True, vmem_limit_bytes=52 << 20
        ),
    )(points, grad_out, counts, mixed)
    out, grad_input, grad_qkv, grad_proj = copy_out(results)
    return out.T, grad_input.T, grad_qkv.transpose(0, 2, 1), grad_proj


def solution(mesh):
    reps = mesh.shape["rep"]
    group = mesh.shape["pts"] // reps
    return jax.shard_map(
        functools.partial(shards, reps, group),
        mesh=mesh,
        in_specs=(
            P("pts", None),
            P("pts"),
            P("pts"),
            P("pts", None),
            P(None, None, "rep"),
            P("rep", None),
        ),
        out_specs=(P("pts", "rep"), P("pts", "rep"), P(None, None, "rep"), P("rep", None)),
        check_vma=False,
    )
```

```python
import functools

import jax
import jax.numpy as jnp
from jax import lax
from jax.experimental import pallas as pl
from jax.experimental.pallas import tpu as pltpu
from jax.sharding import PartitionSpec as P

HEAD = 16
CORES = 2
SCALE = 0.25
EPS = 1e-05
NEGATIVE = -1e30
DEAD = 64.0
ALIVE_BELOW = 32.0
DIGIT = 64
LANES = 128
F32, BF16 = jnp.float32, jnp.bfloat16
MESH = pl.DeviceIdType.MESH
VMEM = pl.BlockSpec(memory_space=pltpu.VMEM)
SMEM = pl.BlockSpec(memory_space=pltpu.SMEM)


def dot(a, b, ca=1, cb=0):
    return lax.dot_general(a, b, (((ca,), (cb,)), ((), ())), preferred_element_type=F32)


def send(src, dst, send_sem, recv_sem, peer):
    copy = pltpu.make_async_remote_copy(
        src_ref=src, dst_ref=dst, send_sem=send_sem, recv_sem=recv_sem,
        device_id=peer, device_id_type=MESH,
    )
    copy.start()
    return copy


def far_first(n):
    return sorted(range(n), key=lambda k: -min(k, n - k))


def pack(array, width, first, group):
    rows = array.shape[0]
    cut = array[:, first : first + width].reshape(group, 2, rows // group // 2, width)
    return jnp.concatenate([cut[:, 0].reshape(rows // 2, width), cut[:, 1].reshape(rows // 2, width)], axis=1)


def unpack(landed, place):
    width = landed.shape[1] // 2
    halves = landed.T
    return dot(jnp.concatenate([halves[:width], halves[width:]], axis=1), place)


def unpack_all(landed, place, depth):
    width = landed.shape[1] // 2
    halves = landed[...].T
    lines = landed.shape[0] // depth
    cuts = [
        halves[width * h : width * (h + 1), lines * zz : lines * (zz + 1)] for zz in range(depth) for h in range(2)
    ]
    return dot(jnp.concatenate(cuts, axis=1), place[...])


def block_kernel(
    reps, group, points_hbm, grads_hbm, counts_ref, mixed_hbm,
    out_ref, gin_ref, gqkv_ref, gproj_ref,
    points, grads, digits, order, target, xs, gs, x_in, g_in, w_all, place,
    qkv, da, bias, scores, at, a_full, dqkv, hbuf, probs, recips,
    pay_out, pay_dx, landed_out, landed_dx,
    core_out, core_in, own, z_out, z_in, row_out, row_all, total,
    load_sems, w_sems, x_sems, g_sems, out_sems, dx_sems,
    core_sems, z_sems, row_sems, all_sems, last_sems,
):
    me, rep = lax.axis_index("pts"), lax.axis_index("rep")
    member = lax.rem(me, group)
    base = me - member
    row = me // group
    slots, channels = points.shape
    patch = x_in.shape[0]
    block = patch // group
    width = channels // reps
    half = 2 * width
    depth = group // CORES
    piece = half // depth
    z, core = member // CORES, lax.rem(member, CORES)
    partner = (base + CORES * z + 1 - core, rep)

    def moved(dz, dc):
        return CORES * lax.rem(z + dz, depth) + lax.rem(core + dc, CORES)

    steps = [(dz, dc) for dz in far_first(depth) for dc in range(CORES)]
    along = [moved(dz, dc) for dz, dc in steps if dz or dc]
    along_z = [lax.rem(z + dz, depth) for dz in far_first(depth) if dz]
    beside = [(me, lax.rem(rep + k, reps)) for k in far_first(reps) if k]
    mates = [
        (lax.rem(rep + k, reps), moved(dz, dc))
        for dz, dc in steps for k in far_first(reps) if k or dz or dc
    ]
    ends = [step for step in steps for k in far_first(reps) if k or step != (0, 0)]
    peers_x = [(lax.rem(row + k, reps) * group + member, rep) for k in far_first(reps) if k]

    w_mine = mixed_hbm.at[0 : 4 * width, :]
    loads = []
    for i, (source, target_ref) in enumerate((
        (mixed_hbm.at[4 * width :, :], digits), (points_hbm, points), (grads_hbm, grads),
        (w_mine, w_all.at[rep]),
    )):
        loads.append(pltpu.make_async_copy(source, target_ref, load_sems.at[i]))
        loads[-1].start()
    barrier = pltpu.get_barrier_semaphore()
    peers = [(base + n, rep) for n in along] + beside + peers_x
    for peer in peers:
        pl.semaphore_signal(barrier, inc=1, device_id=peer, device_id_type=MESH)

    loads[0].wait()
    both = digits[...].astype(F32)
    turned = (both[:, :LANES] * DIGIT + both[:, LANES:]).T
    for j in range(slots // LANES):
        order[LANES * j : LANES * (j + 1), :] = jnp.broadcast_to(turned[:, j : j + 1], (LANES, 8)).astype(jnp.int32)
    rows = order[pl.ds(pl.multiple_of(rep * patch, patch), patch), 0:1]
    live = rows < counts_ref[0]
    slot = lax.broadcasted_iota(jnp.int32, (patch, slots), 1)
    pick = jnp.where(rows == slot, 1.0, 0.0).astype(BF16)
    loads[1].wait()
    xs[...] = jnp.where(live, dot(pick, points[...]), DEAD).astype(BF16)
    pl.semaphore_wait(barrier, len(peers))

    sent, w_copies, x_copies, g_copies = [], [], [], []
    for k, peer in enumerate(beside):
        w_copies.append(send(w_mine, w_all.at[rep], w_sems.at[0, k], w_sems.at[1, k], peer))
    here = pl.ds(pl.multiple_of(member * block, block), block)

    def scatter(staged, landed, sems, copies):
        for k, other in enumerate(along):
            there = pl.ds(pl.multiple_of(other * block, block), block)
            copies.append(
                send(staged.at[there, :], landed.at[here, :], sems.at[0, k], sems.at[1, k], (base + other, rep))
            )
        landed[here, :] = staged[here, :]

    scatter(xs, x_in, x_sems, x_copies)
    loads[2].wait()
    gs[...] = jnp.where(live, dot(pick, grads[...]), 0.0).astype(BF16)

    small = block // 2
    first = 0
    for zz in range(depth):
        for hh in range(2):
            for cc in range(CORES):
                for k in range(reps):
                    start = ((k * depth + zz) * CORES + cc) * block + hh * small
                    target[first : first + small, :] = order[start : start + small, :]
                    first += small
    chunk = 128

    def fill(c, _):
        rows = pl.ds(pl.multiple_of(c * chunk, chunk), chunk)
        arrival = lax.broadcasted_iota(jnp.int32, (chunk, slots), 1)
        place[rows, :] = jnp.where(target[rows, 0:1] == arrival, 1.0, 0.0).astype(BF16)
        return 0

    lax.fori_loop(0, slots // chunk, fill, 0)

    for copy in x_copies:
        copy.wait_recv()
    scatter(gs, g_in, g_sems, g_copies)
    x = x_in[...].astype(F32)
    mu = jnp.mean(x, axis=1, keepdims=True)
    centered = x - mu
    inv = lax.rsqrt(jnp.mean(centered * centered, axis=1, keepdims=True) + EPS)
    hbuf[...] = (centered * inv).astype(BF16)
    keep = x[:, 0:1] < ALIVE_BELOW
    key = lax.broadcasted_iota(jnp.int32, (patch, patch), 0)
    query = lax.broadcasted_iota(jnp.int32, (patch, patch), 1)
    bias[...] = jnp.where(keep | (key == query), 0.0, NEGATIVE)
    loads[3].wait()
    for copy in w_copies:
        copy.wait_recv()
    def weights(first, last):
        return jnp.concatenate(
            [w_all[k, width * i : width * (i + 1), :] for i in range(first, last) for k in range(reps)], axis=0
        )

    projected = dot(weights(0, 3), hbuf[...], 1, 1).astype(BF16)
    qkv[0:channels, :] = (projected[0:channels] * SCALE).astype(BF16)
    qkv[channels:, :] = projected[channels:]
    ones = jnp.ones((HEAD, patch), BF16)

    def heads(n):
        o = pl.multiple_of(n * HEAD, HEAD)
        return (
            pl.ds(o, HEAD), qkv[pl.ds(o, HEAD), :],
            qkv[pl.ds(channels + o, HEAD), :], qkv[pl.ds(2 * channels + o, HEAD), :],
        )

    def score(n):
        _, qh, kh, _ = heads(n)
        return dot(kh, qh, 0, 0) + bias[...]

    def mix(n, s):
        rows, _, _, vh = heads(n)
        e = jnp.exp(s - jnp.max(s, axis=0, keepdims=True)).astype(BF16)
        probs[n] = e
        mixed = dot(jnp.concatenate([vh, ones], axis=0), e)
        recip = 1.0 / mixed[HEAD : HEAD + 1]
        a = mixed[0:HEAD] * recip
        recips[pl.ds(n, 1), :] = recip
        a_full[rows, :] = a
        at[rows, :] = a.astype(BF16)

    count = channels // HEAD
    unrolled = 8

    def forward(i, _):
        for j in range(unrolled):
            n = i * unrolled + j
            follower = lax.rem(n + 1, count) if j == unrolled - 1 else n + 1
            scores[(j + 1) % 2] = score(follower)
            mix(n, scores[j % 2])
        return 0

    scores[0] = score(0)
    lax.fori_loop(0, count // unrolled, forward, 0)
    x = x_in[...].astype(F32)
    out = (keep.astype(F32) * (x + dot(at[...], weights(3, 4), 0, 0))).astype(BF16)
    back = pl.ds(pl.multiple_of((member * reps + rep) * small, small), small)

    def stage(array, pay, landed):
        for r in range(reps):
            pay[r] = pack(array, width, width * r, group)
        landed[back, :] = pay[rep, pl.ds(pl.multiple_of(member * small, small), small), :]

    def give_back(pay, landed, sems, which):
        copies = []
        for i in which:
            k, n = mates[i]
            there = pl.ds(pl.multiple_of(n * small, small), small)
            copies.append(
                send(pay.at[k, there, :], landed.at[back, :], sems.at[0, i], sems.at[1, i], (base + n, k))
            )
        return copies

    stage(out, pay_out, landed_out)
    out_copies = give_back(pay_out, landed_out, out_sems, range(len(mates)))

    for copy in g_copies:
        copy.wait_recv()
    da[...] = dot(weights(3, 4), g_in[...], 1, 1).astype(BF16)

    def backward(n):
        rows, qh, kh, vh = heads(n)
        dahf = da[rows, :].astype(F32) * recips[pl.ds(n, 1), :]
        dah = dahf.astype(BF16)
        delta = jnp.sum(dahf * a_full[rows, :], axis=0, keepdims=True)
        e = probs[n]
        o = pl.multiple_of(n * HEAD, HEAD)
        dp = dot(vh, dah, 0, 0)
        dqkv[pl.ds(2 * channels + o, HEAD), :] = dot(dah, e, 1, 1).astype(BF16)
        ds = (e.astype(F32) * (dp - delta)).astype(BF16)
        dqkv[pl.ds(o, HEAD), :] = (dot(kh, ds) * SCALE).astype(BF16)
        dqkv[pl.ds(channels + o, HEAD), :] = dot(qh, ds, 1, 1).astype(BF16)

    core_copies, z_copies, row_copies = [], [], []
    kept = pl.ds(pl.multiple_of(core * half, half), half)

    def to_core(t):
        core_out[t] = own[t, pl.ds(pl.multiple_of((1 - core) * half, half), half), :].astype(BF16)
        core_copies.append(send(core_out.at[t], core_in.at[t], core_sems.at[0, t], core_sems.at[1, t], partner))

    def to_z(t):
        core_copies[t].wait_recv()
        partial = own[t, kept, :] + core_in[t].astype(F32)
        own[t, 0:half, :] = partial
        z_out[t] = partial.astype(BF16)
        for k, other in enumerate(along_z):
            there = pl.ds(pl.multiple_of(other * piece, piece), piece)
            i = t * (depth - 1) + k
            z_copies.append(
                send(
                    z_out.at[t, there, :], z_in.at[t, k], z_sems.at[0, i], z_sems.at[1, i],
                    (base + CORES * other + core, rep),
                )
            )

    def to_rows(t):
        summed = own[t, pl.ds(pl.multiple_of(z * piece, piece), piece), :]
        for k in range(depth - 1):
            z_copies[t * (depth - 1) + k].wait_recv()
            summed = summed + z_in[t, k].astype(F32)
        row_out[t] = summed
        if t == reps - 1:
            row_all[row, rep] = summed
        for k in far_first(reps):
            if k or t < reps - 1:
                i = t * reps + k
                row_copies.append(
                    send(
                        row_out.at[t], row_all.at[row, rep], row_sems.at[0, i], row_sems.at[1, i],
                        (lax.rem(row + k, reps) * group + member, lax.rem(rep + 1 + t, reps)),
                    )
                )

    per = width // HEAD
    for t in range(reps):
        part = lax.rem(rep + 1 + t, reps)
        for i in range(per):
            backward(part * per + i)
        first = pl.multiple_of(part * width, width)
        grown = [dqkv[pl.ds(channels * i + first, width), :] for i in range(3)]
        own[t, 0 : 3 * width, :] = dot(jnp.concatenate(grown, axis=0), hbuf[...])
        own[t, 3 * width :, :] = dot(at[pl.ds(first, width), :], g_in[...])
        to_core(t)
        if t:
            to_z(t - 1)

    dh = dot(dqkv[...], weights(0, 3), 0, 0)
    xhat = (x_in[...].astype(F32) - mu) * inv
    mean_dh = jnp.mean(dh, axis=1, keepdims=True)
    mean_dot = jnp.mean(dh * xhat, axis=1, keepdims=True)
    to_z(reps - 1)
    dx = (g_in[...].astype(F32) + inv * (dh - mean_dh - xhat * mean_dot)).astype(BF16)
    stage(dx, pay_dx, landed_dx)
    dx_copies = give_back(pay_dx, landed_dx, dx_sems, range(len(mates)))
    for t in range(reps):
        to_rows(t)
    for copy in out_copies:
        copy.wait_recv()
    out_ref[...] = unpack_all(landed_out, place, depth).astype(BF16)
    for copy in row_copies:
        copy.wait_recv()
    summed = row_all[0, 0]
    for k in range(1, reps * reps):
        summed = summed + row_all[k // reps, k % reps]
    done = pl.ds(pl.multiple_of(core * half + z * piece, piece), piece)
    total[done, :] = summed.astype(BF16)
    all_copies = [
        send(
            total.at[done, :], total.at[done, :], all_sems.at[0, k], all_sems.at[1, k],
            (base + CORES * other + core, rep),
        )
        for k, other in enumerate(along_z)
    ]
    span = slots // depth
    lines = group * reps * small // depth
    for dz in reversed(far_first(depth)):
        for copy, (step, _) in zip(dx_copies, ends):
            if step == dz:
                copy.wait_recv()
        source = lax.rem(z + depth - dz, depth)
        landed_rows = landed_dx[pl.ds(pl.multiple_of(source * lines, lines), lines), :]
        part = unpack(landed_rows, place[pl.ds(pl.multiple_of(source * span, span), span), :])
        if dz:
            gin_ref[...] += part
        else:
            gin_ref[...] = part
    for copy in all_copies:
        copy.wait_recv()
    last = send(total.at[kept, :], total.at[kept, :], last_sems.at[0], last_sems.at[1], partner)
    last.wait_recv()
    for i in range(3):
        gqkv_ref[i] = total[width * i : width * (i + 1), :].astype(F32)
    gproj_ref[...] = total[3 * width :, :].astype(F32)
    for copy in (
        w_copies + x_copies + g_copies + out_copies + dx_copies
        + core_copies + z_copies + row_copies + all_copies + [last]
    ):
        copy.wait_send()


def copy_kernel(*refs):
    count = len(refs) // 2
    sources, targets, sems = refs[:count], refs[count : 2 * count], refs[2 * count]
    copies = [pltpu.make_async_copy(a, b, sems.at[i]) for i, (a, b) in enumerate(zip(sources, targets))]
    for copy in copies:
        copy.start()
    for copy in copies:
        copy.wait()


def copy_out(arrays):
    return pl.pallas_call(
        copy_kernel,
        out_shape=[jax.ShapeDtypeStruct(a.shape, a.dtype) for a in arrays],
        in_specs=[pl.BlockSpec(memory_space=pl.ANY)] * len(arrays),
        out_specs=[pl.BlockSpec(memory_space=pl.ANY)] * len(arrays),
        scratch_shapes=[pltpu.SemaphoreType.DMA((len(arrays),))],
        compiler_params=pltpu.CompilerParams(vmem_limit_bytes=1 << 20),
    )(*arrays)


def shards(reps, group, points, counts, order, grad_out, w_qkv, w_proj):
    slots, channels = points.shape
    patch = slots // reps
    width = channels // reps
    half = 2 * width
    piece = half // (group // CORES)
    heads = channels // HEAD
    dma = pltpu.SemaphoreType.DMA
    vmem = pltpu.VMEM
    anywhere = pl.BlockSpec(memory_space=pl.ANY)
    order = order.reshape(-1, LANES)
    digits = jnp.concatenate([order // DIGIT, order % DIGIT], axis=1).astype(BF16)
    digits = jnp.pad(digits, ((0, 16 - digits.shape[0]), (0, 0)))
    mixed = jnp.concatenate([w_qkv.transpose(0, 2, 1).reshape(3 * width, channels), w_proj, digits], axis=0)
    results = pl.pallas_call(
        functools.partial(block_kernel, reps, group),
        out_shape=[
            jax.ShapeDtypeStruct((width, slots), BF16),
            jax.ShapeDtypeStruct((width, slots), F32),
            jax.ShapeDtypeStruct((3, width, channels), F32),
            jax.ShapeDtypeStruct((width, channels), F32),
        ],
        in_specs=[anywhere, anywhere, SMEM, anywhere],
        out_specs=[VMEM] * 4,
        scratch_shapes=[
            vmem((slots, channels), BF16),
            vmem((slots, channels), BF16),
            vmem((16, 2 * LANES), BF16),
            vmem((slots, 8), jnp.int32),
            vmem((slots, 8), jnp.int32),
            vmem((patch, channels), BF16),
            vmem((patch, channels), BF16),
            vmem((patch, channels), BF16),
            vmem((patch, channels), BF16),
            vmem((reps, 4 * width, channels), BF16),
            vmem((slots, slots), BF16),
            vmem((3 * channels, patch), BF16),
            vmem((channels, patch), BF16),
            vmem((patch, patch), F32),
            vmem((2, patch, patch), F32),
            vmem((channels, patch), BF16),
            vmem((channels, patch), F32),
            vmem((3 * channels, patch), BF16),
            vmem((patch, channels), BF16),
            vmem((heads, patch, patch), BF16),
            vmem((heads, patch), F32),
            vmem((reps, patch // 2, 2 * width), BF16),
            vmem((reps, patch // 2, 2 * width), BF16),
            vmem((slots // 2, 2 * width), BF16),
            vmem((slots // 2, 2 * width), BF16),
            vmem((reps, half, channels), BF16),
            vmem((reps, half, channels), BF16),
            vmem((reps, 4 * width, channels), F32),
            vmem((reps, half, channels), BF16),
            vmem((reps, group // CORES - 1, piece, channels), BF16),
            vmem((reps, piece, channels), F32),
            vmem((reps, reps, piece, channels), F32),
            vmem((4 * width, channels), BF16),
            dma((4,)),
            dma((2, reps - 1)),
            dma((2, group - 1)),
            dma((2, group - 1)),
            dma((2, group * reps - 1)),
            dma((2, group * reps - 1)),
            dma((2, reps)),
            dma((2, reps * (group // CORES - 1))),
            dma((2, reps * reps)),
            dma((2, group // CORES - 1)),
            dma((2,)),
        ],
        compiler_params=pltpu.CompilerParams(
            collective_id=0, has_side_effects=True, vmem_limit_bytes=52 << 20
        ),
    )(points, grad_out, counts, mixed)
    out, grad_input, grad_qkv, grad_proj = copy_out(results)
    return out.T, grad_input.T, grad_qkv.transpose(0, 2, 1), grad_proj


def solution(mesh):
    reps = mesh.shape["rep"]
    group = mesh.shape["pts"] // reps
    return jax.shard_map(
        functools.partial(shards, reps, group),
        mesh=mesh,
        in_specs=(
            P("pts", None),
            P("pts"),
            P("pts"),
            P("pts", None),
            P(None, None, "rep"),
            P("rep", None),
        ),
        out_specs=(P("pts", "rep"), P("pts", "rep"), P(None, None, "rep"), P("rep", None)),
        check_vma=False,
    )
```
